32 devices in a mesh: expert: 4 (over z), seq: 4 (over x, core), fsdp: 2 (over y).
Axes of the slice: x: 2, y: 2, z: 4, core: 2. Of those that a mesh axis runs over, the one named last changes fastest.
Arguments:
- tokens: float32 [7168, 1280], P(('expert', 'seq', 'fsdp')), may hold values from -100 to 100
- slot_params: float32 [1280, 32], replicated, may hold values from -4 to 4
- w_in: float32 [8, 2560, 1280], P('expert', ('seq', 'fsdp')), may hold values from -0.15625 to 0.15625
- w_out: float32 [8, 2560, 1280], P('expert', ('seq', 'fsdp')), may hold values from -0.125 to 0.125
Outputs:
- mixed: float32 [7168, 1280], P(('expert', 'seq', 'fsdp'))
The draws below stay inside these ranges and needn't reach their ends.
All inputs are finite; a program needn't handle non-finite values.
Results may differ from the reference program's by a relative error of at most 0.0003.
Values sent between devices are 32-bit elements; how exact they have to be, the bound alone decides.
No kernel may reach another device: no remote copies, remote signals or barrier semaphores. Data moves between devices by JAX's collectives and lax.ppermute only.
A program may use at most 64 MiB of HBM per device.

```python
import math
import jax
import jax.numpy as jnp
from jax import lax

D = 1280
MLP = 2560
SLOTS = 4
EXPERTS = 8
TOKENS = 7168


def slot_matrix(key):
    folded = jax.random.fold_in(key, 11)
    keys = jax.random.split(folded, 2)
    columns = EXPERTS * SLOTS
    gains = jnp.exp(jax.random.uniform(keys[0], (1, columns), jnp.float32, math.log(3.0), math.log(6.0)))
    values_drawn = jnp.clip(jax.random.normal(keys[1], (D, columns), jnp.float32), -5.0, 5.0)
    return values_drawn * gains / math.sqrt(D)


def draw_slot_params(key, part):
    return slot_matrix(key)


def draw_tokens(key, part):
    folded = jax.random.fold_in(key, 23)
    keys = jax.random.split(folded, 1)
    values_drawn = jnp.clip(jax.random.normal(keys[0], (TOKENS, D), jnp.float32), -6.0, 6.0)
    return values_drawn


def level_of(own_key, shape, shards, smallest, top_value):
    factor_of = 1.0
    for dim, blocks in shards:
        draws = jax.random.uniform(jax.random.fold_in(jax.random.fold_in(own_key, 6), dim), (blocks,), jnp.float32, smallest / len(shards), top_value / len(shards))
        factor_of = factor_of * jnp.repeat(jnp.exp(draws), shape[dim] // blocks).reshape((-1,) + (1,) * (len(shape) - 1 - dim))
    return factor_of


def gaussian(own_key, dims, scale, bound, cuts=(), kind=jnp.bfloat16):
    loudness = level_of(own_key, dims, cuts, -0.22, 0.18) if cuts else 1.0
    array = jax.random.normal(own_key, dims, jnp.float32) * scale * loudness
    return jnp.minimum(jnp.maximum(array, -bound), bound).astype(kind)


def setup_inputs(seed: int = 0) -> dict:
    splits = jax.random.split(jax.random.key(seed), 5)
    tokens = draw_tokens(jax.random.fold_in(splits[4], 71), 0)
    slot_params = draw_slot_params(jax.random.fold_in(splits[4], 71), 0)
    w_in = gaussian(splits[2], (EXPERTS, MLP, D), D ** -0.5, 0.15625, ((0, 4), (1, 8)), jnp.float32)
    w_out = gaussian(splits[3], (EXPERTS, MLP, D), MLP ** -0.5, 0.125, ((0, 4), (1, 8)), jnp.float32)
    return dict(tokens=tokens, slot_params=slot_params, w_in=w_in, w_out=w_out)


def reference(tokens, slot_params, w_in, w_out):
    highest = lax.Precision.HIGHEST
    logits = jnp.dot(tokens, slot_params, precision=highest, preferred_element_type=jnp.float32)
    slot_peak = jnp.max(logits, axis=0, keepdims=True)
    weights = jnp.exp(logits - slot_peak)
    slot_mass = jnp.sum(weights, axis=0)
    slot_sums = jnp.dot(weights.T, tokens, precision=highest, preferred_element_type=jnp.float32)
    slot_inputs = (slot_sums / slot_mass[:, None]).reshape(EXPERTS, SLOTS, D)
    hidden = jax.nn.gelu(jnp.einsum("esd,ehd->esh", slot_inputs, w_in, precision=highest), approximate=False)
    slot_outputs = jnp.einsum("esh,ehd->esd", hidden, w_out, precision=highest).reshape(EXPERTS * SLOTS, D)
    row_peak = jnp.max(logits, axis=1, keepdims=True)
    row_exp = jnp.exp(logits - row_peak)
    combine = row_exp / jnp.sum(row_exp, axis=1, keepdims=True)
    return jnp.dot(combine, slot_outputs, precision=highest, preferred_element_type=jnp.float32)
```

```python
import functools

import jax
import jax.numpy as jnp
from jax import lax
from jax.experimental import pallas as pl
from jax.experimental.pallas import tpu as pltpu
from jax.sharding import PartitionSpec as P

SLOTS = 4
LANES = 128
AXES = ("expert", "seq", "fsdp")
VMEM = pl.BlockSpec(memory_space=pltpu.VMEM)
SMEM = pl.BlockSpec(memory_space=pltpu.SMEM)


def pieces(value, count):
    out = []
    for _ in range(count):
        part = value.astype(jnp.bfloat16)
        out.append(part)
        value = value - part.astype(jnp.float32)
    return out


def mm(left, right, contract=((1,), (0,))):
    return lax.dot_general(left, right, (contract, ((), ())), preferred_element_type=jnp.float32)


def pick(core, when_zero, when_one):
    return jnp.where(core == 0, when_zero, when_one)


def dispatch_kernel(core_ref, tokens_ref, params_ref, logits_ref, mine_ref, theirs_ref):
    core = core_ref[0]
    groups, tiles, rows, _ = mine_ref.shape
    half = tiles - 2
    slots = params_ref.shape[1]
    count = tokens_ref.shape[0]
    token_parts = pieces(tokens_ref[...], 3)
    param_parts = pieces(params_ref[...], 3)
    products = mm(jnp.concatenate(token_parts, axis=0), jnp.concatenate(param_parts, axis=1))

    def term(i, j):
        return products[i * count:(i + 1) * count, j * slots:(j + 1) * slots]

    small = term(0, 2) + term(1, 1) + term(2, 0)
    logits = (small + (term(0, 1) + term(1, 0))) + term(0, 0)
    logits = logits.T
    logits_ref[...] = logits
    peak = jnp.max(logits, axis=1, keepdims=True)
    weights = jnp.exp(logits - peak)
    mass = jnp.sum(weights, axis=1, keepdims=True)
    weight_parts = pieces(weights, 2)
    high = mm(jnp.concatenate(weight_parts, axis=0), token_parts[0])
    sums = high[:slots] + (high[slots:] + mm(weight_parts[0], token_parts[1]))
    peak = jnp.broadcast_to(peak, (slots, LANES))
    mass = jnp.broadcast_to(mass, (slots, LANES))
    for g in range(groups):
        own = slice(g * rows, (g + 1) * rows)
        for t in range(half):
            first = sums[own, t * LANES:(t + 1) * LANES]
            second = sums[own, (t + half) * LANES:(t + half + 1) * LANES]
            mine_ref[g, t] = pick(core, first, second)
            theirs_ref[g, t] = pick(core, second, first)
        for ref in (mine_ref, theirs_ref):
            ref[g, half] = mass[own]
            ref[g, half + 1] = peak[own]


def combine_kernel(logits_ref, out_ref):
    logits = logits_ref[...]
    top = jnp.max(logits, axis=0, keepdims=True)
    powers = jnp.exp(logits - top)
    combine = (powers / jnp.sum(powers, axis=0, keepdims=True)).T
    high, low = pieces(combine, 2)
    out_ref[...] = jnp.concatenate([high, low, high], axis=1)


def expert_kernel(core_ref, mine_ref, theirs_ref, w_in_ref, w_out_ref, own_ref, send_ref):
    core = core_ref[0]
    half = own_ref.shape[0]
    rows = own_ref.shape[1]
    experts, units, width = w_in_ref.shape
    mine = [mine_ref[t] / mine_ref[half] for t in range(half)]
    theirs = [theirs_ref[t] / theirs_ref[half] for t in range(half)]
    first = [pick(core, a, b) for a, b in zip(mine, theirs)]
    second = [pick(core, b, a) for a, b in zip(mine, theirs)]
    inputs = jnp.concatenate(first + second, axis=1)
    high, low = pieces(inputs, 2)
    both = jnp.concatenate([high.astype(jnp.float32), low.astype(jnp.float32)], axis=0).astype(jnp.bfloat16)
    w_high, w_low = pieces(w_in_ref[...].reshape(experts * units, width), 2)
    nt = ((1,), (1,))
    large = mm(w_high, both, nt).T
    small = mm(w_low, both, nt).T
    value = large[:rows] + (large[rows:] + small[:rows])
    value = value * (1.0 + lax.erf(value * (0.5 ** 0.5))) * 0.5
    slot = lax.broadcasted_iota(jnp.int32, value.shape, 0)
    unit = lax.broadcasted_iota(jnp.int32, value.shape, 1)
    keep = None
    for e in range(experts):
        inside = (slot // SLOTS == e) & (unit >= e * units) & (unit < (e + 1) * units)
        keep = inside if keep is None else keep | inside
    value = jnp.where(keep, value, 0.0)
    high, low = pieces(value, 2)
    both = jnp.concatenate([high.astype(jnp.float32), low.astype(jnp.float32)], axis=0).astype(jnp.bfloat16)
    w_high, w_low = pieces(w_out_ref[...].reshape(experts * units, width), 2)
    large = mm(both, w_high)
    small = mm(both, w_low)
    out = large[:rows] + (large[rows:] + small[:rows])
    for t in range(half):
        first = out[:, t * LANES:(t + 1) * LANES]
        second = out[:, (t + half) * LANES:(t + half + 1) * LANES]
        own_ref[t] = pick(core, first, second)
        send_ref[t] = pick(core, second, first)


def mix_kernel(core_ref, combine_ref, mine_ref, theirs_ref, out_ref, stack_ref):
    core, expert = core_ref[0], core_ref[1]
    groups, half, rows, _ = mine_ref.shape
    slots = groups * rows
    for k in range(groups):
        place = pl.ds(pl.multiple_of((expert ^ k) * rows, rows), rows)
        for t in range(half):
            stack_ref[place, t * LANES:(t + 1) * LANES] = pick(core, mine_ref[k, t], theirs_ref[k, t])
            stack_ref[place, (t + half) * LANES:(t + half + 1) * LANES] = pick(core, theirs_ref[k, t], mine_ref[k, t])
    high, low = pieces(stack_ref[...], 2)
    out_ref[...] = mm(combine_ref[...], jnp.concatenate([high, high, low], axis=0))


def join(parts, axis):
    size = parts[0].shape[axis] - 1
    peaks = [lax.slice_in_dim(p, size, size + 1, axis=axis) for p in parts]
    top = functools.reduce(jnp.maximum, peaks)
    total = sum(lax.slice_in_dim(p, 0, size, axis=axis) * jnp.exp(q - top) for p, q in zip(parts, peaks))
    return jnp.concatenate([total, top], axis=axis)


def solution(mesh):
    n_expert, n_seq, n_fsdp = (mesh.shape[a] for a in AXES)
    n_x = n_seq // 2

    def permute(value, target):
        pairs = []
        for e in range(n_expert):
            for s in range(n_seq):
                for f in range(n_fsdp):
                    te, tx, tc, tf = target(e, s // 2, s % 2, f)
                    pairs.append(((e * n_seq + s) * n_fsdp + f, (te * n_seq + tx * 2 + tc) * n_fsdp + tf))
        return lax.ppermute(value, AXES, pairs)

    def other_core(value):
        return permute(value, lambda e, x, c, f: (e, x, 1 - c, f))

    def along_expert(value, k):
        return permute(value, lambda e, x, c, f: (e ^ k, x, c, f))

    def plane(value):
        return [
            permute(value, lambda e, x, c, f, dx=dx, df=df: (e, (x + dx) % n_x, c, (f + df) % n_fsdp))
            for dx in range(n_x) for df in range(n_fsdp) if dx or df
        ]

    def body(tokens, slot_params, w_in, w_out):
        count, width = tokens.shape
        slots = slot_params.shape[1]
        rows = w_in.shape[0] * SLOTS
        half = width // LANES // 2
        f32 = jnp.float32
        params = pltpu.CompilerParams(vmem_limit_bytes=24 * 1024 * 1024)
        expert = lax.axis_index("expert")
        place = jnp.stack([lax.axis_index("seq") % 2, expert]).astype(jnp.int32)

        shape = jax.ShapeDtypeStruct((n_expert, half + 2, rows, LANES), f32)
        logits, mine, theirs = pl.pallas_call(
            dispatch_kernel,
            out_shape=(jax.ShapeDtypeStruct((slots, count), f32), shape, shape),
            in_specs=[SMEM, VMEM, VMEM],
            out_specs=(VMEM, VMEM, VMEM),
            compiler_params=params,
        )(place, tokens, slot_params)
        combine = pl.pallas_call(
            combine_kernel,
            out_shape=jax.ShapeDtypeStruct((count, 3 * slots), jnp.bfloat16),
            in_specs=[VMEM],
            out_specs=VMEM,
            compiler_params=params,
        )(logits)

        chip = join([mine, other_core(theirs)], 1)
        at = lambda k: lax.dynamic_index_in_dim(chip, expert ^ k, 0, keepdims=False)
        total = join([at(0)] + [along_expert(at(k), k) for k in range(1, n_expert)], 0)
        total = join([total] + plane(total), 0)
        shape = jax.ShapeDtypeStruct((half, rows, LANES), f32)
        own, send = pl.pallas_call(
            expert_kernel,
            out_shape=(shape, shape),
            in_specs=[SMEM, VMEM, VMEM, VMEM, VMEM],
            out_specs=(VMEM, VMEM),
            compiler_params=params,
        )(place, total, other_core(total), w_in, w_out)
        own = own + other_core(send)
        own = own + sum(plane(own))
        gathered = jnp.stack([own] + [along_expert(own, k) for k in range(1, n_expert)])
        block = 256 if width % 256 == 0 else width
        return pl.pallas_call(
            mix_kernel,
            out_shape=jax.ShapeDtypeStruct((count, width), f32),
            in_specs=[SMEM, VMEM, VMEM, VMEM],
            out_specs=VMEM,
            scratch_shapes=[pltpu.VMEM((slots, width), f32)],
            compiler_params=params,
        )(place, combine, gathered, other_core(gathered))

    return jax.shard_map(
        body,
        mesh=mesh,
        in_specs=(P(AXES, None), P(), P("expert", ("seq", "fsdp"), None), P("expert", ("seq", "fsdp"), None)),
        out_specs=P(AXES, None),
        check_vma=False,
    )
```

```python
import functools

import jax
import jax.numpy as jnp
from jax import lax
from jax.experimental import pallas as pl
from jax.experimental.pallas import tpu as pltpu
from jax.sharding import PartitionSpec as P

SLOTS = 4
LANES = 128
AXES = ("expert", "seq", "fsdp")
VMEM = pl.BlockSpec(memory_space=pltpu.VMEM)
SMEM = pl.BlockSpec(memory_space=pltpu.SMEM)
HBM = pl.BlockSpec(memory_space=pltpu.HBM)


def pieces(value, count):
    out = []
    for _ in range(count):
        part = value.astype(jnp.bfloat16)
        out.append(part)
        value = value - part.astype(jnp.float32)
    return out


def stacked(value):
    high, low = pieces(value, 2)
    return jnp.concatenate([high.astype(jnp.float32), low.astype(jnp.float32)], axis=0).astype(jnp.bfloat16)


def mm(left, right, contract=((1,), (0,))):
    return lax.dot_general(left, right, (contract, ((), ())), preferred_element_type=jnp.float32)


def pick(core, when_zero, when_one):
    return jnp.where(core == 0, when_zero, when_one)


def join(parts):
    top = functools.reduce(jnp.maximum, [p[-1] for p in parts])
    total = sum(p[:-1] * jnp.exp(p[-1] - top)[None] for p in parts)
    return jnp.concatenate([total, top[None]], axis=0)


def dispatch_kernel(chunks, place_ref, tokens_hbm, params_hbm, w_in_hbm, w_out_hbm,
                    logits_ref, mine_ref, theirs_ref, w_in_ref, w_out_ref,
                    tokens_ref, params_ref, sums_ref, sems):
    core, expert = place_ref[0], place_ref[1]
    groups, tiles, rows, _ = mine_ref.shape
    half = tiles - 2
    slots, _ = params_hbm.shape
    count = tokens_hbm.shape[0] // chunks
    params_copy = pltpu.make_async_copy(params_hbm, params_ref, sems.at[chunks])
    params_copy.start()
    copies = []
    for i in range(chunks):
        own = pl.ds(i * count, count)
        copies.append(pltpu.make_async_copy(tokens_hbm.at[own], tokens_ref.at[own], sems.at[i]))
        copies[i].start()
    weight_copies = [
        pltpu.make_async_copy(w_in_hbm, w_in_ref, sems.at[chunks + 1]),
        pltpu.make_async_copy(w_out_hbm, w_out_ref, sems.at[chunks + 2]),
    ]
    for copy in weight_copies:
        copy.start()
    params_copy.wait()
    params = jnp.concatenate(pieces(params_ref[...], 3), axis=0)
    highs, lows, logits = [], [], []
    for i in range(chunks):
        copies[i].wait()
        parts = pieces(tokens_ref[i * count:(i + 1) * count], 3)
        highs.append(parts[0])
        lows.append(parts[1])
        products = mm(jnp.concatenate(parts, axis=0), params, ((1,), (1,)))

        def term(i, j):
            return products[i * count:(i + 1) * count, j * slots:(j + 1) * slots]

        small = term(0, 2) + term(1, 1) + term(2, 0)
        logits.append((small + (term(0, 1) + term(1, 0))) + term(0, 0))
    logits = jnp.concatenate(logits, axis=0).T
    logits_ref[...] = logits
    peak = jnp.max(logits, axis=1, keepdims=True)
    weights = jnp.exp(logits - peak)
    mass = jnp.sum(weights, axis=1, keepdims=True)
    weight_high, weight_low = pieces(weights, 2)
    high = mm(jnp.concatenate([weight_high, weight_low], axis=0), jnp.concatenate(highs, axis=0))
    low = mm(weight_high, jnp.concatenate(lows, axis=0))
    width = high.shape[1]
    sums_ref[:, :width] = high[:slots] + (high[slots:] + low)
    sums_ref[:, width:width + LANES] = jnp.broadcast_to(mass, (slots, LANES))
    sums_ref[:, width + LANES:] = jnp.broadcast_to(peak, (slots, LANES))
    for k in range(groups):
        own = pl.ds(pl.multiple_of((expert ^ k) * rows, rows), rows)
        first, second = (mine_ref, theirs_ref) if k else (theirs_ref, mine_ref)
        for t in range(half):
            one = sums_ref[own, t * LANES:(t + 1) * LANES]
            two = sums_ref[own, (t + half) * LANES:(t + half + 1) * LANES]
            first[k, t] = pick(core, one, two)
            second[k, t] = pick(core, two, one)
        for t in range(2):
            value = sums_ref[own, width + t * LANES:width + (t + 1) * LANES]
            mine_ref[k, half + t] = value
            theirs_ref[k, half + t] = value
    for copy in weight_copies:
        copy.wait()


def chip_kernel(mine_ref, theirs_ref, *outs):
    for k, out_ref in enumerate(outs):
        out_ref[...] = join([mine_ref[k], theirs_ref[k]])


def combine_kernel(logits_ref, out_ref):
    logits = logits_ref[...]
    top = jnp.max(logits, axis=0, keepdims=True)
    powers = jnp.exp(logits - top)
    combine = (powers / jnp.sum(powers, axis=0, keepdims=True)).T
    high, low = pieces(combine, 2)
    out_ref[...] = jnp.concatenate([high, low, high], axis=1)


def expert_kernel(place_ref, sent_ref, got_ref, w_in_ref, w_out_ref, out_ref):
    core = place_ref[0]
    tiles, rows, _ = out_ref.shape
    half = tiles // 2
    experts, units, width = w_in_ref.shape
    near = join([sent_ref[0], got_ref[1]])
    far = join([sent_ref[1], got_ref[0]])
    near = [near[t] / near[half] for t in range(half)]
    far = [far[t] / far[half] for t in range(half)]
    first = [pick(core, a, b) for a, b in zip(near, far)]
    second = [pick(core, b, a) for a, b in zip(near, far)]
    inputs = stacked(jnp.concatenate(first + second, axis=1))
    w_high, w_low = pieces(w_in_ref[...].reshape(experts * units, width), 2)
    nt = ((1,), (1,))
    large = mm(w_high, inputs, nt).T
    small = mm(w_low, inputs, nt).T
    value = large[:rows] + (large[rows:] + small[:rows])
    value = value * (1.0 + lax.erf(value * (0.5 ** 0.5))) * 0.5
    slot = lax.broadcasted_iota(jnp.int32, value.shape, 0)
    unit = lax.broadcasted_iota(jnp.int32, value.shape, 1)
    keep = None
    for e in range(experts):
        inside = (slot // SLOTS == e) & (unit >= e * units) & (unit < (e + 1) * units)
        keep = inside if keep is None else keep | inside
    hidden = stacked(jnp.where(keep, value, 0.0))
    w_high, w_low = pieces(w_out_ref[...].reshape(experts * units, width), 2)
    large = mm(hidden, w_high)
    small = mm(hidden, w_low)
    out = large[:rows] + (large[rows:] + small[:rows])
    for t in range(tiles):
        out_ref[t] = out[:, t * LANES:(t + 1) * LANES]


def mix_kernel(near, place_ref, combine_ref, own_ref, others_ref, *refs):
    out_hbm, slots_ref, out_ref, sems = refs[-4:]
    core, expert = place_ref[0], place_ref[1]
    half, rows, _ = own_ref.shape
    groups = others_ref.shape[0] + 1
    for k in range(groups):
        place = pl.ds(pl.multiple_of((expert ^ k) * rows, rows), rows)
        for t in range(half):
            slots_ref[place, t * LANES:(t + 1) * LANES] = others_ref[k - 1, t] if k else own_ref[t]
    high, low = pieces(slots_ref[...], 2)
    out_ref[...] = mm(combine_ref[...], jnp.concatenate([high, high, low], axis=0))
    side = core if near else 1 - core
    columns = pl.ds(pl.multiple_of(side * (half * LANES), LANES), half * LANES)
    copy = pltpu.make_async_copy(out_ref, out_hbm.at[:, columns], sems)
    copy.start()
    copy.wait()


def solution(mesh):
    n_expert, n_seq, n_fsdp = (mesh.shape[a] for a in AXES)
    n_x = n_seq // 2

    def permute(value, target):
        pairs = []
        for e in range(n_expert):
            for s in range(n_seq):
                for f in range(n_fsdp):
                    te, tx, tc, tf = target(e, s // 2, s % 2, f)
                    pairs.append(((e * n_seq + s) * n_fsdp + f, (te * n_seq + tx * 2 + tc) * n_fsdp + tf))
        return lax.ppermute(value, AXES, pairs)

    def other_core(value):
        return permute(value, lambda e, x, c, f: (e, x, 1 - c, f))

    def along_expert(value, k):
        return permute(value, lambda e, x, c, f: (e ^ k, x, 1 - c, f))

    def plane(value):
        return [
            permute(value, lambda e, x, c, f, dx=dx, df=df: (e, (x + dx) % n_x, 1 - c, (f + df) % n_fsdp))
            for dx in range(n_x) for df in range(n_fsdp) if dx or df
        ]

    def body(tokens, slot_params, w_in, w_out):
        count, width = tokens.shape
        slots = slot_params.shape[1]
        rows = w_in.shape[0] * SLOTS
        half = width // LANES // 2
        f32 = jnp.float32
        params = pltpu.CompilerParams(vmem_limit_bytes=24 * 1024 * 1024)
        core = lax.axis_index("seq") % 2
        place = jnp.stack([core, lax.axis_index("expert")]).astype(jnp.int32)
        chunks = 2 if count % 32 == 0 else 1

        in_hbm = lambda value: pltpu.with_memory_space_constraint(value, pltpu.HBM)
        shape = pltpu.VMEM((n_expert, half + 2, rows, LANES), f32)
        logits, mine, theirs, w_in, w_out = pl.pallas_call(
            functools.partial(dispatch_kernel, chunks),
            out_shape=(pltpu.VMEM((slots, count), f32), shape, shape, pltpu.VMEM(w_in.shape, f32), pltpu.VMEM(w_out.shape, f32)),
            in_specs=[SMEM, HBM, HBM, HBM, HBM],
            out_specs=(VMEM,) * 5,
            scratch_shapes=[
                pltpu.VMEM((count, width), f32),
                pltpu.VMEM((slots, width), f32),
                pltpu.VMEM((slots, width + 2 * LANES), f32),
                pltpu.SemaphoreType.DMA((chunks + 3,)),
            ],
            compiler_params=params,
        )(place, in_hbm(tokens), in_hbm(slot_params.T), in_hbm(w_in), in_hbm(w_out))
        combine = pl.pallas_call(
            combine_kernel,
            out_shape=jax.ShapeDtypeStruct((count, 3 * slots), jnp.bfloat16),
            in_specs=[VMEM],
            out_specs=VMEM,
            compiler_params=params,
        )(logits)

        chip = pl.pallas_call(
            chip_kernel,
            out_shape=(pltpu.VMEM((half + 2, rows, LANES), f32),) * n_expert,
            in_specs=[VMEM, VMEM],
            out_specs=(VMEM,) * n_expert,
            compiler_params=params,
        )(mine, other_core(theirs))
        total = join([chip[0]] + [along_expert(chip[k], k) for k in range(1, n_expert)])
        sent = jnp.stack([join(plane(total)), total])
        partial = pl.pallas_call(
            expert_kernel,
            out_shape=jax.ShapeDtypeStruct((2 * half, rows, LANES), f32),
            in_specs=[SMEM, VMEM, VMEM, VMEM, VMEM],
            out_specs=VMEM,
            compiler_params=params,
        )(place, sent, other_core(sent), w_in, w_out)
        partial = partial + other_core(partial)
        first, second = partial[:half], partial[half:]
        own = pick(core, second, first) + sum(plane(pick(core, first, second)))
        others = jnp.stack([along_expert(own, k) for k in range(1, n_expert)])

        def mix(near, own, others, *out):
            return pl.pallas_call(
                functools.partial(mix_kernel, near),
                out_shape=jax.ShapeDtypeStruct((count, width), f32),
                in_specs=[SMEM, VMEM, VMEM, VMEM] + [HBM] * len(out),
                out_specs=HBM,
                scratch_shapes=[
                    pltpu.VMEM((slots, half * LANES), f32),
                    pltpu.VMEM((count, half * LANES), f32),
                    pltpu.SemaphoreType.DMA,
                ],
                input_output_aliases={4: 0} if out else {},
                compiler_params=params,
            )(place, combine, own, others, *out)

        mixed = mix(True, other_core(own), others)
        return mix(False, own, other_core(others), mixed)

    return jax.shard_map(
        body,
        mesh=mesh,
        in_specs=(P(AXES, None), P(), P("expert", ("seq", "fsdp"), None), P("expert", ("seq", "fsdp"), None)),
        out_specs=P(AXES, None),
        check_vma=False,
    )
```

```python
import functools

import jax
import jax.numpy as jnp
from jax import lax
from jax.experimental import pallas as pl
from jax.experimental.pallas import tpu as pltpu
from jax.sharding import PartitionSpec as P

SLOTS = 4
LANES = 128
AXES = ("expert", "seq", "fsdp")
VMEM = pl.BlockSpec(memory_space=pltpu.VMEM)
HBM = pl.BlockSpec(memory_space=pltpu.HBM)


def pieces(value, count):
    out = []
    for _ in range(count):
        part = value.astype(jnp.bfloat16)
        out.append(part)
        value = value - part.astype(jnp.float32)
    return out


def stacked(value):
    high, low = pieces(value, 2)
    return jnp.concatenate([high.astype(jnp.float32), low.astype(jnp.float32)], axis=0).astype(jnp.bfloat16)


def mm(left, right, contract=((1,), (0,))):
    return lax.dot_general(left, right, (contract, ((), ())), preferred_element_type=jnp.float32)


def pick(core, when_zero, when_one):
    return jnp.where(core == 0, when_zero, when_one)


def join(parts):
    top = functools.reduce(jnp.maximum, [p[-1] for p in parts])
    total = sum(p[:-1] * jnp.exp(p[-1] - top)[None] for p in parts)
    return jnp.concatenate([total, top[None]], axis=0)


def dispatch_kernel(chunks, tokens_hbm, params_hbm, w_in_hbm, logits_ref, mine_ref, theirs_ref, w_in_ref,
                    tokens_ref, params_ref, sums_ref, sems):
    core, expert = lax.axis_index("seq") % 2, lax.axis_index("expert")
    groups, tiles, rows, _ = mine_ref.shape
    half = tiles - 2
    slots, width = params_hbm.shape
    copies = [pltpu.make_async_copy(params_hbm, params_ref, sems.at[0])]
    for start, stop in chunks:
        own = pl.ds(start, stop - start)
        copies.append(pltpu.make_async_copy(tokens_hbm.at[own], tokens_ref.at[own], sems.at[len(copies)]))
    copies.append(pltpu.make_async_copy(w_in_hbm, w_in_ref, sems.at[len(copies)]))
    for copy in copies:
        copy.start()
    copies[0].wait()
    params = jnp.concatenate(pieces(params_ref[...], 3), axis=0)
    highs, lows, logits = [], [], []
    nt = ((1,), (1,))
    for (start, stop), copy in zip(chunks, copies[1:]):
        copy.wait()
        high, low, rest = pieces(tokens_ref[start:stop], 3)
        highs.append(high)
        lows.append(low)
        a = mm(params, high, nt)
        b = mm(params[:2 * slots], low, nt)
        c = mm(params[:slots], rest, nt)
        small = a[2 * slots:] + b[slots:] + c
        logits.append((small + (a[slots:2 * slots] + b[:slots])) + a[:slots])
    logits = jnp.concatenate(logits, axis=1)
    logits_ref[...] = logits
    peak = jnp.max(logits, axis=1, keepdims=True)
    weights = jnp.exp(logits - peak)
    mass = jnp.sum(weights, axis=1, keepdims=True)
    weight_high, weight_low = pieces(weights, 2)
    high = mm(jnp.concatenate([weight_high, weight_low], axis=0), jnp.concatenate(highs, axis=0))
    low = mm(weight_high, jnp.concatenate(lows, axis=0))
    sums_ref[:, :width] = high[:slots] + (high[slots:] + low)
    sums_ref[:, width:width + LANES] = jnp.broadcast_to(mass, (slots, LANES))
    sums_ref[:, width + LANES:] = jnp.broadcast_to(peak, (slots, LANES))
    for k in range(groups):
        own = pl.ds(pl.multiple_of((expert ^ k) * rows, rows), rows)
        sides = (core, 1 - core) if k else (1 - core, core)
        for ref, side in zip((mine_ref, theirs_ref), sides):
            for t in range(half):
                place = pl.ds(pl.multiple_of((side * half + t) * LANES, LANES), LANES)
                ref[k, t] = sums_ref[own, place]
            for t in range(2):
                ref[k, half + t] = sums_ref[own, width + t * LANES:width + (t + 1) * LANES]
    copies[-1].wait()


def chip_kernel(mine_ref, theirs_ref, *outs):
    for k, out_ref in enumerate(outs):
        out_ref[...] = join([mine_ref[k], theirs_ref[k]])


def split_out_kernel(_, w_hbm, high_ref, low_ref, flag_ref, w_ref, sems):
    experts, units, _ = w_hbm.shape
    parts = sems.shape[0] // experts
    count = units // parts
    copies = []
    for e in range(experts):
        for i in range(parts):
            own = pl.ds(i * count, count)
            copies.append(pltpu.make_async_copy(w_hbm.at[e, own], w_ref.at[e, own], sems.at[len(copies)]))
            copies[-1].start()
    for e in range(experts):
        for i in range(parts):
            copies[e * parts + i].wait()
            start = e * units + i * count
            own = slice(start, start + count)
            high_ref[own], low_ref[own] = pieces(w_ref[e, i * count:(i + 1) * count], 2)
    flag_ref[...] = jnp.zeros_like(flag_ref)


def split_in_kernel(_, w_ref, high_ref, low_ref, flag_ref):
    experts, units, width = w_ref.shape
    high, low = pieces(w_ref[...].reshape(experts * units, width), 2)
    high_ref[...] = high.T
    low_ref[...] = low.T
    flag_ref[...] = jnp.zeros_like(flag_ref)


def total_kernel(own_ref, *refs):
    *others, _, out_ref = refs
    out_ref[...] = join([own_ref[...]] + [r[...] for r in others])


def plane_kernel(own_ref, *refs):
    *others, _, out_ref = refs
    out_ref[0] = join([r[...] for r in others])
    out_ref[1] = own_ref[...]


def stack_kernel(_, *refs):
    *others, out_ref = refs
    for k, r in enumerate(others):
        out_ref[k] = r[...]


def combine_kernel(logits_ref, out_ref):
    logits = logits_ref[...]
    top = jnp.max(logits, axis=0, keepdims=True)
    powers = jnp.exp(logits - top)
    combine = (powers / jnp.sum(powers, axis=0, keepdims=True)).T
    high, low = pieces(combine, 2)
    out_ref[...] = jnp.concatenate([high, low, high], axis=1)


def expert_kernel(sent_ref, got_ref, in_high_ref, in_low_ref, out_high_ref, out_low_ref, out_ref):
    core = lax.axis_index("seq") % 2
    tiles, rows, _ = out_ref.shape
    half = tiles // 2
    experts = rows // SLOTS
    units = in_high_ref.shape[1] // experts
    near = join([sent_ref[0], got_ref[1]])
    far = join([sent_ref[1], got_ref[0]])
    near = [near[t] / near[half] for t in range(half)]
    far = [far[t] / far[half] for t in range(half)]
    first = [pick(core, a, b) for a, b in zip(near, far)]
    second = [pick(core, b, a) for a, b in zip(near, far)]
    inputs = stacked(jnp.concatenate(first + second, axis=1))
    large = mm(inputs, in_high_ref[...])
    small = mm(inputs, in_low_ref[...])
    value = large[:rows] + (large[rows:] + small[:rows])
    value = value * (1.0 + lax.erf(value * (0.5 ** 0.5))) * 0.5
    slot = lax.broadcasted_iota(jnp.int32, value.shape, 0)
    unit = lax.broadcasted_iota(jnp.int32, value.shape, 1)
    keep = None
    for e in range(experts):
        inside = (slot // SLOTS == e) & (unit >= e * units) & (unit < (e + 1) * units)
        keep = inside if keep is None else keep | inside
    hidden = stacked(jnp.where(keep, value, 0.0))
    large = mm(hidden, out_high_ref[...])
    small = mm(hidden, out_low_ref[...])
    out = large[:rows] + (large[rows:] + small[:rows])
    for t in range(tiles):
        out_ref[t] = out[:, t * LANES:(t + 1) * LANES]


def mix_kernel(near, combine_ref, own_ref, others_ref, *refs):
    out_hbm, slots_ref, out_ref, sems = refs[-4:]
    core, expert = lax.axis_index("seq") % 2, lax.axis_index("expert")
    half, rows, _ = own_ref.shape
    groups = others_ref.shape[0] + 1
    for k in range(groups):
        place = pl.ds(pl.multiple_of((expert ^ k) * rows, rows), rows)
        for t in range(half):
            slots_ref[place, t * LANES:(t + 1) * LANES] = others_ref[k - 1, t] if k else own_ref[t]
    high, low = pieces(slots_ref[...], 2)
    slots = jnp.concatenate([high, high, low], axis=0)
    side = core if near else 1 - core
    columns = pl.ds(pl.multiple_of(side * (half * LANES), LANES), half * LANES)
    parts = sems.shape[0]
    count = combine_ref.shape[0] // parts
    copies = []
    for i in range(parts):
        own = slice(i * count, (i + 1) * count)
        out_ref[own] = mm(combine_ref[own], slots)
        place = pl.ds(i * count, count)
        copies.append(pltpu.make_async_copy(out_ref.at[place], out_hbm.at[place, columns], sems.at[i]))
        copies[i].start()
    for copy in copies:
        copy.wait()


def solution(mesh):
    n_expert, n_seq, n_fsdp = (mesh.shape[a] for a in AXES)
    n_x = n_seq // 2

    def permute(value, target):
        pairs = []
        for e in range(n_expert):
            for s in range(n_seq):
                for f in range(n_fsdp):
                    te, tx, tc, tf = target(e, s // 2, s % 2, f)
                    pairs.append(((e * n_seq + s) * n_fsdp + f, (te * n_seq + tx * 2 + tc) * n_fsdp + tf))
        return lax.ppermute(value, AXES, pairs)

    def other_core(value):
        return permute(value, lambda e, x, c, f: (e, x, 1 - c, f))

    def along_expert(value, k):
        return permute(value, lambda e, x, c, f: (e ^ k, x, 1 - c, f))

    def plane(value):
        return [
            permute(value, lambda e, x, c, f, dx=dx, df=df: (e, (x + dx) % n_x, 1 - c, (f + df) % n_fsdp))
            for dx in range(n_x) for df in range(n_fsdp) if dx or df
        ]

    def body(tokens, slot_params, w_in, w_out):
        count, width = tokens.shape
        slots = slot_params.shape[1]
        rows = w_in.shape[0] * SLOTS
        half = width // LANES // 2
        f32 = jnp.float32
        params = pltpu.CompilerParams(vmem_limit_bytes=24 * 1024 * 1024)
        core = lax.axis_index("seq") % 2
        chunks = [(i, min(i + LANES, count)) for i in range(0, count, LANES)]

        in_hbm = lambda value: pltpu.with_memory_space_constraint(value, pltpu.HBM)
        shape = pltpu.VMEM((n_expert, half + 2, rows, LANES), f32)
        logits, mine, theirs, w_in = pl.pallas_call(
            functools.partial(dispatch_kernel, chunks),
            out_shape=(pltpu.VMEM((slots, count), f32), shape, shape, pltpu.VMEM(w_in.shape, f32)),
            in_specs=[HBM, HBM, HBM],
            out_specs=(VMEM,) * 4,
            scratch_shapes=[
                pltpu.VMEM((count, width), f32),
                pltpu.VMEM((slots, width), f32),
                pltpu.VMEM((slots, width + 2 * LANES), f32),
                pltpu.SemaphoreType.DMA((len(chunks) + 2,)),
            ],
            compiler_params=params,
        )(in_hbm(tokens), in_hbm(slot_params.T), in_hbm(w_in))
        combine = pl.pallas_call(
            combine_kernel,
            out_shape=jax.ShapeDtypeStruct((count, 3 * slots), jnp.bfloat16),
            in_specs=[VMEM],
            out_specs=VMEM,
            compiler_params=params,
        )(logits)

        chip = pl.pallas_call(
            chip_kernel,
            out_shape=(pltpu.VMEM((half + 2, rows, LANES), f32),) * n_expert,
            in_specs=[VMEM, VMEM],
            out_specs=(VMEM,) * n_expert,
            compiler_params=params,
        )(mine, other_core(theirs))
        order = list(range(n_expert - 1, 0, -1))
        flag = pltpu.VMEM((8, LANES), f32)
        experts, units, _ = w_in.shape
        cost = pl.CostEstimate(flops=8 * w_in.size, bytes_accessed=8 * w_in.size, transcendentals=0)

        def local(kernel, out, *args):
            return pl.pallas_call(
                kernel, out_shape=out, in_specs=[VMEM] * len(args), out_specs=VMEM, compiler_params=params
            )(*args)

        part = pltpu.VMEM((experts * units, width), jnp.bfloat16)
        parts = 4 if units % 64 == 0 else 1
        out_high, out_low, ready = pl.pallas_call(
            split_out_kernel,
            out_shape=(part, part, flag),
            in_specs=[VMEM, HBM],
            out_specs=(VMEM,) * 3,
            scratch_shapes=[pltpu.VMEM(w_out.shape, f32), pltpu.SemaphoreType.DMA((experts * parts,))],
            cost_estimate=cost,
            compiler_params=params,
        )(chip[0], in_hbm(w_out))
        shape = pltpu.VMEM((half + 2, rows, LANES), f32)
        total = local(total_kernel, shape, chip[0], *[along_expert(chip[k], k) for k in order], ready)
        part = pltpu.VMEM((width, experts * units), jnp.bfloat16)
        in_high, in_low, ready = pl.pallas_call(
            split_in_kernel,
            out_shape=(part, part, flag),
            in_specs=[VMEM, VMEM],
            out_specs=(VMEM,) * 3,
            cost_estimate=cost,
            compiler_params=params,
        )(total, w_in)
        shape = pltpu.VMEM((2, half + 2, rows, LANES), f32)
        sent = local(plane_kernel, shape, total, *plane(total), ready)
        shape = pltpu.VMEM((2 * half, rows, LANES), f32)
        partial = local(expert_kernel, shape, sent, other_core(sent), in_high, in_low, out_high, out_low)
        partial = partial + other_core(partial)
        first, second = partial[:half], partial[half:]
        own = pick(core, second, first) + sum(plane(pick(core, first, second)))
        arrived = {k: along_expert(own, k) for k in order}
        own_near = other_core(own)
        shape = pltpu.VMEM((n_expert - 1, half, rows, LANES), f32)
        others = local(stack_kernel, shape, own_near, *[arrived[k] for k in range(1, n_expert)])

        def mix(near, own, others, *out):
            return pl.pallas_call(
                functools.partial(mix_kernel, near),
                out_shape=jax.ShapeDtypeStruct((count, width), f32),
                in_specs=[VMEM, VMEM, VMEM] + [HBM] * len(out),
                out_specs=HBM,
                scratch_shapes=[
                    pltpu.VMEM((slots, half * LANES), f32),
                    pltpu.VMEM((count, half * LANES), f32),
                    pltpu.SemaphoreType.DMA((2 if count % 32 == 0 else 1,)),
                ],
                input_output_aliases={3: 0} if out else {},
                compiler_params=params,
            )(combine, own, others, *out)

        mixed = mix(True, own_near, others)
        return mix(False, own, other_core(others), mixed)

    return jax.shard_map(
        body,
        mesh=mesh,
        in_specs=(P(AXES, None), P(), P("expert", ("seq", "fsdp"), None), P("expert", ("seq", "fsdp"), None)),
        out_specs=P(AXES, None),
        check_vma=False,
    )
```

```python
import functools

import jax
import jax.numpy as jnp
from jax import lax
from jax.experimental import pallas as pl
from jax.experimental.pallas import tpu as pltpu
from jax.sharding import PartitionSpec as P

SLOTS = 4
LANES = 128
AXES = ("expert", "seq", "fsdp")
VMEM = pl.BlockSpec(memory_space=pltpu.VMEM)
HBM = pl.BlockSpec(memory_space=pltpu.HBM)


def pieces(value, count):
    out = []
    for _ in range(count):
        part = value.astype(jnp.bfloat16)
        out.append(part)
        value = value - part.astype(jnp.float32)
    return out


def stacked(value):
    high, low = pieces(value, 2)
    return jnp.concatenate([high.astype(jnp.float32), low.astype(jnp.float32)], axis=0).astype(jnp.bfloat16)


def mm(left, right, contract=((1,), (0,))):
    return lax.dot_general(left, right, (contract, ((), ())), preferred_element_type=jnp.float32)


def pick(core, when_zero, when_one):
    return jnp.where(core == 0, when_zero, when_one)


def join(parts):
    top = functools.reduce(jnp.maximum, [p[-1] for p in parts])
    total = sum(p[:-1] * jnp.exp(p[-1] - top)[None] for p in parts)
    return jnp.concatenate([total, top[None]], axis=0)


def dispatch_kernel(chunks, tokens_hbm, params_hbm, w_in_hbm, logits_ref, mine_ref, theirs_ref, w_in_ref,
                    tokens_ref, params_ref, sums_ref, sems):
    core, expert = lax.axis_index("seq") % 2, lax.axis_index("expert")
    groups, tiles, rows, _ = mine_ref.shape
    half = tiles - 2
    slots, width = params_hbm.shape
    copies = [pltpu.make_async_copy(params_hbm, params_ref, sems.at[0])]
    for start, stop in chunks:
        own = pl.ds(start, stop - start)
        copies.append(pltpu.make_async_copy(tokens_hbm.at[own], tokens_ref.at[own], sems.at[len(copies)]))
    copies.append(pltpu.make_async_copy(w_in_hbm, w_in_ref, sems.at[len(copies)]))
    for copy in copies:
        copy.start()
    copies[0].wait()
    params = jnp.concatenate(pieces(params_ref[...], 3), axis=0)
    highs, lows, logits = [], [], []
    nt = ((1,), (1,))
    for (start, stop), copy in zip(chunks, copies[1:]):
        copy.wait()
        high, low, rest = pieces(tokens_ref[start:stop], 3)
        highs.append(high)
        lows.append(low)
        a = mm(params, high, nt)
        b = mm(params[:2 * slots], low, nt)
        c = mm(params[:slots], rest, nt)
        small = a[2 * slots:] + b[slots:] + c
        logits.append((small + (a[slots:2 * slots] + b[:slots])) + a[:slots])
    logits = jnp.concatenate(logits, axis=1)
    logits_ref[...] = logits
    peak = jnp.max(logits, axis=1, keepdims=True)
    weights = jnp.exp(logits - peak)
    mass = jnp.sum(weights, axis=1, keepdims=True)
    weight_high, weight_low = pieces(weights, 2)
    high = mm(jnp.concatenate([weight_high, weight_low], axis=0), jnp.concatenate(highs, axis=0))
    low = mm(weight_high, jnp.concatenate(lows, axis=0))
    sums_ref[:, :width] = high[:slots] + (high[slots:] + low)
    sums_ref[:, width:width + LANES] = jnp.broadcast_to(mass, (slots, LANES))
    sums_ref[:, width + LANES:] = jnp.broadcast_to(peak, (slots, LANES))
    for k in range(groups):
        own = pl.ds(pl.multiple_of((expert ^ k) * rows, rows), rows)
        sides = (core, 1 - core) if k else (1 - core, core)
        for ref, side in zip((mine_ref, theirs_ref), sides):
            for t in range(half):
                place = pl.ds(pl.multiple_of((side * half + t) * LANES, LANES), LANES)
                ref[k, t] = sums_ref[own, place]
            for t in range(2):
                ref[k, half + t] = sums_ref[own, width + t * LANES:width + (t + 1) * LANES]
    copies[-1].wait()


def chip_kernel(mine_ref, theirs_ref, *outs):
    for k, out_ref in enumerate(outs):
        out_ref[...] = join([mine_ref[k], theirs_ref[k]])


def split_out_kernel(_, w_hbm, high_ref, low_ref, flag_ref, w_ref, sems):
    experts, units, _ = w_hbm.shape
    parts = sems.shape[0] // experts
    count = units // parts
    copies = []
    for e in range(experts):
        for i in range(parts):
            own = pl.ds(i * count, count)
            copies.append(pltpu.make_async_copy(w_hbm.at[e, own], w_ref.at[e, own], sems.at[len(copies)]))
            copies[-1].start()
    for e in range(experts):
        for i in range(parts):
            copies[e * parts + i].wait()
            start = e * units + i * count
            own = slice(start, start + count)
            high_ref[own], low_ref[own] = pieces(w_ref[e, i * count:(i + 1) * count], 2)
    flag_ref[...] = jnp.zeros_like(flag_ref)


def split_in_kernel(_, w_ref, high_ref, low_ref, flag_ref):
    experts, units, width = w_ref.shape
    high, low = pieces(w_ref[...].reshape(experts * units, width), 2)
    high_ref[...] = high.T
    low_ref[...] = low.T
    flag_ref[...] = jnp.zeros_like(flag_ref)


def total_kernel(own_ref, *refs):
    *others, _, out_ref = refs
    out_ref[...] = join([own_ref[...]] + [r[...] for r in others])


def plane_kernel(own_ref, *refs):
    *others, _, out_ref = refs
    out_ref[0] = join([r[...] for r in others])
    out_ref[1] = own_ref[...]


def stack_kernel(*refs):
    _, _, *others, out_ref = refs
    for k, r in enumerate(reversed(others)):
        out_ref[k] = r[...]


def combine_kernel(logits_ref, out_ref):
    logits = logits_ref[...]
    top = jnp.max(logits, axis=0, keepdims=True)
    powers = jnp.exp(logits - top)
    combine = (powers / jnp.sum(powers, axis=0, keepdims=True)).T
    high, low = pieces(combine, 2)
    out_ref[...] = jnp.concatenate([high, low, high], axis=1)


def expert_kernel(sent_ref, got_ref, in_high_ref, in_low_ref, out_high_ref, out_low_ref, out_ref):
    core = lax.axis_index("seq") % 2
    tiles, rows, _ = out_ref.shape
    half = tiles // 2
    experts = rows // SLOTS
    units = in_high_ref.shape[1] // experts
    near = join([sent_ref[0], got_ref[1]])
    far = join([sent_ref[1], got_ref[0]])
    near = [near[t] / near[half] for t in range(half)]
    far = [far[t] / far[half] for t in range(half)]
    first = [pick(core, a, b) for a, b in zip(near, far)]
    second = [pick(core, b, a) for a, b in zip(near, far)]
    inputs = stacked(jnp.concatenate(first + second, axis=1))
    large = mm(inputs, in_high_ref[...])
    small = mm(inputs, in_low_ref[...])
    value = large[:rows] + (large[rows:] + small[:rows])
    value = value * (1.0 + lax.erf(value * (0.5 ** 0.5))) * 0.5
    slot = lax.broadcasted_iota(jnp.int32, value.shape, 0)
    unit = lax.broadcasted_iota(jnp.int32, value.shape, 1)
    keep = None
    for e in range(experts):
        inside = (slot // SLOTS == e) & (unit >= e * units) & (unit < (e + 1) * units)
        keep = inside if keep is None else keep | inside
    hidden = stacked(jnp.where(keep, value, 0.0))
    large = mm(hidden, out_high_ref[...])
    small = mm(hidden, out_low_ref[...])
    out = large[:rows] + (large[rows:] + small[:rows])
    for t in range(tiles):
        out_ref[t] = out[:, t * LANES:(t + 1) * LANES]


def mix_kernel(near, combine_ref, own_ref, others_ref, *refs):
    out_hbm, slots_ref, out_ref, sems = refs[-4:]
    core, expert = lax.axis_index("seq") % 2, lax.axis_index("expert")
    half, rows, _ = own_ref.shape
    groups = others_ref.shape[0] + 1
    for k in range(groups):
        place = pl.ds(pl.multiple_of((expert ^ k) * rows, rows), rows)
        for t in range(half):
            slots_ref[place, t * LANES:(t + 1) * LANES] = others_ref[k - 1, t] if k else own_ref[t]
    high, low = pieces(slots_ref[...], 2)
    slots = jnp.concatenate([high, high, low], axis=0)
    side = core if near else 1 - core
    columns = pl.ds(pl.multiple_of(side * (half * LANES), LANES), half * LANES)
    parts = sems.shape[0]
    count = combine_ref.shape[0] // parts
    copies = []
    for i in range(parts):
        own = slice(i * count, (i + 1) * count)
        out_ref[own] = mm(combine_ref[own], slots)
        place = pl.ds(i * count, count)
        copies.append(pltpu.make_async_copy(out_ref.at[place], out_hbm.at[place, columns], sems.at[i]))
        copies[i].start()
    for copy in copies:
        copy.wait()


def solution(mesh):
    n_expert, n_seq, n_fsdp = (mesh.shape[a] for a in AXES)
    n_x = n_seq // 2

    def permute(value, target):
        pairs = []
        for e in range(n_expert):
            for s in range(n_seq):
                for f in range(n_fsdp):
                    te, tx, tc, tf = target(e, s // 2, s % 2, f)
                    pairs.append(((e * n_seq + s) * n_fsdp + f, (te * n_seq + tx * 2 + tc) * n_fsdp + tf))
        return lax.ppermute(value, AXES, pairs)

    def other_core(value):
        return permute(value, lambda e, x, c, f: (e, x, 1 - c, f))

    def along_expert(value, k):
        return permute(value, lambda e, x, c, f: (e ^ k, x, 1 - c, f))

    def plane(value):
        return [
            permute(value, lambda e, x, c, f, dx=dx, df=df: (e, (x + dx) % n_x, 1 - c, (f + df) % n_fsdp))
            for dx in range(n_x) for df in range(n_fsdp) if dx or df
        ]

    def body(tokens, slot_params, w_in, w_out):
        count, width = tokens.shape
        slots = slot_params.shape[1]
        rows = w_in.shape[0] * SLOTS
        half = width // LANES // 2
        f32 = jnp.float32
        params = pltpu.CompilerParams(vmem_limit_bytes=24 * 1024 * 1024)
        core = lax.axis_index("seq") % 2
        chunks = [(0, count)]
        in_hbm = lambda value: pltpu.with_memory_space_constraint(value, pltpu.HBM)
        shape = pltpu.VMEM((n_expert, half + 2, rows, LANES), f32)
        logits, mine, theirs, w_in = pl.pallas_call(
            functools.partial(dispatch_kernel, chunks),
            out_shape=(pltpu.VMEM((slots, count), f32), shape, shape, pltpu.VMEM(w_in.shape, f32)),
            in_specs=[HBM, HBM, HBM],
            out_specs=(VMEM,) * 4,
            scratch_shapes=[
                pltpu.VMEM((count, width), f32),
                pltpu.VMEM((slots, width), f32),
                pltpu.VMEM((slots, width + 2 * LANES), f32),
                pltpu.SemaphoreType.DMA((len(chunks) + 2,)),
            ],
            compiler_params=params,
        )(in_hbm(tokens), in_hbm(slot_params.T), in_hbm(w_in))
        combine = pl.pallas_call(
            combine_kernel,
            out_shape=jax.ShapeDtypeStruct((count, 3 * slots), jnp.bfloat16),
            in_specs=[VMEM],
            out_specs=VMEM,
            compiler_params=params,
        )(logits)

        chip = pl.pallas_call(
            chip_kernel,
            out_shape=(pltpu.VMEM((half + 2, rows, LANES), f32),) * n_expert,
            in_specs=[VMEM, VMEM],
            out_specs=(VMEM,) * n_expert,
            compiler_params=params,
        )(mine, other_core(theirs))
        order = list(range(n_expert - 1, 0, -1))
        flag = pltpu.VMEM((8, LANES), f32)
        experts, units, _ = w_in.shape
        cost = pl.CostEstimate(flops=8 * w_in.size, bytes_accessed=8 * w_in.size, transcendentals=0)

        def local(kernel, out, *args):
            return pl.pallas_call(
                kernel, out_shape=out, in_specs=[VMEM] * len(args), out_specs=VMEM, compiler_params=params
            )(*args)

        part = pltpu.VMEM((experts * units, width), jnp.bfloat16)
        parts = 4 if units % 64 == 0 else 1
        out_high, out_low, ready = pl.pallas_call(
            split_out_kernel,
            out_shape=(part, part, flag),
            in_specs=[VMEM, HBM],
            out_specs=(VMEM,) * 3,
            scratch_shapes=[pltpu.VMEM(w_out.shape, f32), pltpu.SemaphoreType.DMA((experts * parts,))],
            cost_estimate=cost,
            compiler_params=params,
        )(chip[0], in_hbm(w_out))
        shape = pltpu.VMEM((half + 2, rows, LANES), f32)
        total = local(total_kernel, shape, chip[0], *[along_expert(chip[k], k) for k in order], ready)
        part = pltpu.VMEM((width, experts * units), jnp.bfloat16)
        in_high, in_low, ready = pl.pallas_call(
            split_in_kernel,
            out_shape=(part, part, flag),
            in_specs=[VMEM, VMEM],
            out_specs=(VMEM,) * 3,
            cost_estimate=cost,
            compiler_params=params,
        )(total, w_in)
        shape = pltpu.VMEM((2, half + 2, rows, LANES), f32)
        sent = local(plane_kernel, shape, total, *plane(total), ready)
        shape = pltpu.VMEM((2 * half, rows, LANES), f32)
        partial = local(expert_kernel, shape, sent, other_core(sent), in_high, in_low, out_high, out_low)
        partial = partial + other_core(partial)
        first, second = partial[:half], partial[half:]
        own = pick(core, second, first) + sum(plane(pick(core, first, second)))
        arrived = [along_expert(own, k) for k in order]
        own_near = other_core(own)
        shape = pltpu.VMEM((n_expert - 1, half, rows, LANES), f32)
        others = local(stack_kernel, shape, combine, own_near, *arrived)

        def mix(near, own, others, *out):
            return pl.pallas_call(
                functools.partial(mix_kernel, near),
                out_shape=jax.ShapeDtypeStruct((count, width), f32),
                in_specs=[VMEM, VMEM, VMEM] + [HBM] * len(out),
                out_specs=HBM,
                scratch_shapes=[
                    pltpu.VMEM((slots, half * LANES), f32),
                    pltpu.VMEM((count, half * LANES), f32),
                    pltpu.SemaphoreType.DMA((2 if count % 32 == 0 else 1,)),
                ],
                input_output_aliases={3: 0} if out else {},
                compiler_params=params,
            )(combine, own, others, *out)

        mixed = mix(True, own_near, others)
        return mix(False, own, other_core(others), mixed)

    return jax.shard_map(
        body,
        mesh=mesh,
        in_specs=(P(AXES, None), P(), P("expert", ("seq", "fsdp"), None), P("expert", ("seq", "fsdp"), None)),
        out_specs=P(AXES, None),
        check_vma=False,
    )
```

```python
import functools

import jax
import jax.numpy as jnp
from jax import lax
from jax.experimental import pallas as pl
from jax.experimental.pallas import tpu as pltpu
from jax.sharding import PartitionSpec as P

SLOTS = 4
LANES = 128
AXES = ("expert", "seq", "fsdp")
VMEM = pl.BlockSpec(memory_space=pltpu.VMEM)
HBM = pl.BlockSpec(memory_space=pltpu.HBM)


def pieces(value, count):
    out = []
    for _ in range(count):
        part = value.astype(jnp.bfloat16)
        out.append(part)
        value = value - part.astype(jnp.float32)
    return out


def stacked(value):
    high, low = pieces(value, 2)
    return jnp.concatenate([high.astype(jnp.float32), low.astype(jnp.float32)], axis=0).astype(jnp.bfloat16)


def mm(left, right, contract=((1,), (0,))):
    return lax.dot_general(left, right, (contract, ((), ())), preferred_element_type=jnp.float32)


def pick(core, when_zero, when_one):
    return jnp.where(core == 0, when_zero, when_one)


def join(parts):
    top = functools.reduce(jnp.maximum, [p[-1] for p in parts])
    total = sum(p[:-1] * jnp.exp(p[-1] - top)[None] for p in parts)
    return jnp.concatenate([total, top[None]], axis=0)


def dispatch_kernel(chunks, tokens_hbm, params_hbm, w_in_hbm, logits_ref, mine_ref, theirs_ref, w_in_ref,
                    tokens_ref, params_ref, sums_ref, sems):
    core, expert = lax.axis_index("seq") % 2, lax.axis_index("expert")
    groups, tiles, rows, _ = mine_ref.shape
    half = tiles - 2
    slots, width = params_hbm.shape
    copies = [pltpu.make_async_copy(params_hbm, params_ref, sems.at[0])]
    for start, stop in chunks:
        own = pl.ds(start, stop - start)
        copies.append(pltpu.make_async_copy(tokens_hbm.at[own], tokens_ref.at[own], sems.at[len(copies)]))
    copies.append(pltpu.make_async_copy(w_in_hbm, w_in_ref, sems.at[len(copies)]))
    for copy in copies:
        copy.start()
    copies[0].wait()
    params = jnp.concatenate(pieces(params_ref[...], 3), axis=0)
    highs, lows, logits = [], [], []
    nt = ((1,), (1,))
    for (start, stop), copy in zip(chunks, copies[1:]):
        copy.wait()
        high, low, rest = pieces(tokens_ref[start:stop], 3)
        highs.append(high)
        lows.append(low)
        a = mm(params, high, nt)
        b = mm(params[:2 * slots], low, nt)
        c = mm(params[:slots], rest, nt)
        small = a[2 * slots:] + b[slots:] + c
        logits.append((small + (a[slots:2 * slots] + b[:slots])) + a[:slots])
    logits = jnp.concatenate(logits, axis=1)
    logits_ref[...] = logits
    peak = jnp.max(logits, axis=1, keepdims=True)
    weights = jnp.exp(logits - peak)
    mass = jnp.sum(weights, axis=1, keepdims=True)
    weight_high, weight_low = pieces(weights, 2)
    high = mm(jnp.concatenate([weight_high, weight_low], axis=0), jnp.concatenate(highs, axis=0))
    low = mm(weight_high, jnp.concatenate(lows, axis=0))
    sums_ref[:, :width] = high[:slots] + (high[slots:] + low)
    sums_ref[:, width:width + LANES] = jnp.broadcast_to(mass, (slots, LANES))
    sums_ref[:, width + LANES:] = jnp.broadcast_to(peak, (slots, LANES))
    for k in range(groups):
        own = pl.ds(pl.multiple_of((expert ^ k) * rows, rows), rows)
        sides = (core, 1 - core) if k else (1 - core, core)
        for ref, side in zip((mine_ref, theirs_ref), sides):
            for t in range(half):
                place = pl.ds(pl.multiple_of((side * half + t) * LANES, LANES), LANES)
                ref[k, t] = sums_ref[own, place]
            for t in range(2):
                ref[k, half + t] = sums_ref[own, width + t * LANES:width + (t + 1) * LANES]
    copies[-1].wait()


def chip_kernel(mine_ref, theirs_ref, *outs):
    for k, out_ref in enumerate(outs):
        out_ref[...] = join([mine_ref[k], theirs_ref[k]])


def split_out_kernel(_, w_hbm, high_ref, low_ref, flag_ref, w_ref, sems):
    experts, units, _ = w_hbm.shape
    parts = sems.shape[0] // experts
    count = units // parts
    copies = []
    for e in range(experts):
        for i in range(parts):
            own = pl.ds(i * count, count)
            copies.append(pltpu.make_async_copy(w_hbm.at[e, own], w_ref.at[e, own], sems.at[len(copies)]))
            copies[-1].start()
    for e in range(experts):
        for i in range(parts):
            copies[e * parts + i].wait()
            start = e * units + i * count
            own = slice(start, start + count)
            high_ref[own], low_ref[own] = pieces(w_ref[e, i * count:(i + 1) * count], 2)
    flag_ref[...] = jnp.zeros_like(flag_ref)


def split_in_kernel(_, w_ref, high_ref, low_ref, flag_ref):
    experts, units, width = w_ref.shape
    high, low = pieces(w_ref[...].reshape(experts * units, width), 2)
    high_ref[...] = high.T
    low_ref[...] = low.T
    flag_ref[...] = jnp.zeros_like(flag_ref)


def total_kernel(own_ref, *refs):
    *others, _, out_ref = refs
    out_ref[...] = join([own_ref[...]] + [r[...] for r in others])


def plane_kernel(own_ref, *refs):
    *others, _, out_ref = refs
    out_ref[0] = join([r[...] for r in others])
    out_ref[1] = own_ref[...]


def stack_kernel(*refs):
    _, *others, _, out_ref = refs
    for k, r in enumerate(reversed(others)):
        out_ref[k] = r[...]


def combine_kernel(logits_ref, out_ref):
    logits = logits_ref[...]
    top = jnp.max(logits, axis=0, keepdims=True)
    powers = jnp.exp(logits - top)
    combine = (powers / jnp.sum(powers, axis=0, keepdims=True)).T
    high, low = pieces(combine, 2)
    out_ref[...] = jnp.concatenate([high, low, high], axis=1)


def expert_kernel(sent_ref, got_ref, in_high_ref, in_low_ref, out_high_ref, out_low_ref, out_ref):
    core = lax.axis_index("seq") % 2
    tiles, rows, _ = out_ref.shape
    half = tiles // 2
    experts = rows // SLOTS
    units = in_high_ref.shape[1] // experts
    near = join([sent_ref[0], got_ref[1]])
    far = join([sent_ref[1], got_ref[0]])
    near = [near[t] / near[half] for t in range(half)]
    far = [far[t] / far[half] for t in range(half)]
    first = [pick(core, a, b) for a, b in zip(near, far)]
    second = [pick(core, b, a) for a, b in zip(near, far)]
    inputs = stacked(jnp.concatenate(first + second, axis=1))
    large = mm(inputs, in_high_ref[...])
    small = mm(inputs, in_low_ref[...])
    value = large[:rows] + (large[rows:] + small[:rows])
    value = value * (1.0 + lax.erf(value * (0.5 ** 0.5))) * 0.5
    slot = lax.broadcasted_iota(jnp.int32, value.shape, 0)
    unit = lax.broadcasted_iota(jnp.int32, value.shape, 1)
    keep = None
    for e in range(experts):
        inside = (slot // SLOTS == e) & (unit >= e * units) & (unit < (e + 1) * units)
        keep = inside if keep is None else keep | inside
    hidden = stacked(jnp.where(keep, value, 0.0))
    large = mm(hidden, out_high_ref[...])
    small = mm(hidden, out_low_ref[...])
    out = large[:rows] + (large[rows:] + small[:rows])
    for t in range(tiles):
        out_ref[t] = out[:, t * LANES:(t + 1) * LANES]


def mix_kernel(near, combine_ref, own_ref, others_ref, *refs):
    out_hbm, slots_ref, out_ref, sems = refs[-4:]
    core, expert = lax.axis_index("seq") % 2, lax.axis_index("expert")
    half, rows, _ = own_ref.shape
    groups = others_ref.shape[0] + 1
    for k in range(groups):
        place = pl.ds(pl.multiple_of((expert ^ k) * rows, rows), rows)
        for t in range(half):
            slots_ref[place, t * LANES:(t + 1) * LANES] = others_ref[k - 1, t] if k else own_ref[t]
    high, low = pieces(slots_ref[...], 2)
    slots = jnp.concatenate([high, high, low], axis=0)
    side = core if near else 1 - core
    columns = pl.ds(pl.multiple_of(side * (half * LANES), LANES), half * LANES)
    count = combine_ref.shape[0]
    step = pl.cdiv(count, 16 * sems.shape[0]) * 16
    copies = []
    for i, start in enumerate(range(0, count, step)):
        size = min(step, count - start)
        out_ref[start:start + size] = mm(combine_ref[start:start + size], slots)
        place = pl.ds(start, size)
        copies.append(pltpu.make_async_copy(out_ref.at[place], out_hbm.at[place, columns], sems.at[i]))
        copies[i].start()
    for copy in copies:
        copy.wait()


def solution(mesh):
    n_expert, n_seq, n_fsdp = (mesh.shape[a] for a in AXES)
    n_x = n_seq // 2

    def permute(value, target):
        pairs = []
        for e in range(n_expert):
            for s in range(n_seq):
                for f in range(n_fsdp):
                    te, tx, tc, tf = target(e, s // 2, s % 2, f)
                    pairs.append(((e * n_seq + s) * n_fsdp + f, (te * n_seq + tx * 2 + tc) * n_fsdp + tf))
        return lax.ppermute(value, AXES, pairs)

    def other_core(value):
        return permute(value, lambda e, x, c, f: (e, x, 1 - c, f))

    def along_expert(value, k):
        return permute(value, lambda e, x, c, f: (e ^ k, x, 1 - c, f))

    def plane(value):
        return [
            permute(value, lambda e, x, c, f, dx=dx, df=df: (e, (x + dx) % n_x, 1 - c, (f + df) % n_fsdp))
            for dx in range(n_x)[::-1] for df in range(n_fsdp)[::-1] if dx or df
        ]

    def body(tokens, slot_params, w_in, w_out):
        count, width = tokens.shape
        slots = slot_params.shape[1]
        rows = w_in.shape[0] * SLOTS
        half = width // LANES // 2
        f32 = jnp.float32
        params = pltpu.CompilerParams(vmem_limit_bytes=24 * 1024 * 1024)
        core = lax.axis_index("seq") % 2
        chunks = [(0, count)]
        in_hbm = lambda value: pltpu.with_memory_space_constraint(value, pltpu.HBM)
        shape = pltpu.VMEM((n_expert, half + 2, rows, LANES), f32)
        logits, mine, theirs, w_in = pl.pallas_call(
            functools.partial(dispatch_kernel, chunks),
            out_shape=(pltpu.VMEM((slots, count), f32), shape, shape, pltpu.VMEM(w_in.shape, f32)),
            in_specs=[HBM, HBM, HBM],
            out_specs=(VMEM,) * 4,
            scratch_shapes=[
                pltpu.VMEM((count, width), f32),
                pltpu.VMEM((slots, width), f32),
                pltpu.VMEM((slots, width + 2 * LANES), f32),
                pltpu.SemaphoreType.DMA((len(chunks) + 2,)),
            ],
            compiler_params=params,
        )(in_hbm(tokens), in_hbm(slot_params.T), in_hbm(w_in))
        combine = pl.pallas_call(
            combine_kernel,
            out_shape=jax.ShapeDtypeStruct((count, 3 * slots), jnp.bfloat16),
            in_specs=[VMEM],
            out_specs=VMEM,
            compiler_params=params,
        )(logits)

        chip = pl.pallas_call(
            chip_kernel,
            out_shape=(pltpu.VMEM((half + 2, rows, LANES), f32),) * n_expert,
            in_specs=[VMEM, VMEM],
            out_specs=(VMEM,) * n_expert,
            compiler_params=params,
        )(mine, other_core(theirs))
        order = list(range(n_expert - 1, 0, -1))
        flag = pltpu.VMEM((8, LANES), f32)
        experts, units, _ = w_in.shape
        cost = pl.CostEstimate(flops=8 * w_in.size, bytes_accessed=8 * w_in.size, transcendentals=0)

        def local(kernel, out, *args):
            return pl.pallas_call(
                kernel, out_shape=out, in_specs=[VMEM] * len(args), out_specs=VMEM, compiler_params=params
            )(*args)

        part = pltpu.VMEM((experts * units, width), jnp.bfloat16)
        parts = 4 if units % 64 == 0 else 1
        out_high, out_low, ready = pl.pallas_call(
            split_out_kernel,
            out_shape=(part, part, flag),
            in_specs=[VMEM, HBM],
            out_specs=(VMEM,) * 3,
            scratch_shapes=[pltpu.VMEM(w_out.shape, f32), pltpu.SemaphoreType.DMA((experts * parts,))],
            cost_estimate=cost,
            compiler_params=params,
        )(chip[0], in_hbm(w_out))
        shape = pltpu.VMEM((half + 2, rows, LANES), f32)
        total = local(total_kernel, shape, chip[0], *[along_expert(chip[k], k) for k in order], ready)
        part = pltpu.VMEM((width, experts * units), jnp.bfloat16)
        in_high, in_low, ready = pl.pallas_call(
            split_in_kernel,
            out_shape=(part, part, flag),
            in_specs=[VMEM, VMEM],
            out_specs=(VMEM,) * 3,
            cost_estimate=cost,
            compiler_params=params,
        )(total, w_in)
        shape = pltpu.VMEM((2, half + 2, rows, LANES), f32)
        sent = local(plane_kernel, shape, total, *plane(total), ready)
        shape = pltpu.VMEM((2 * half, rows, LANES), f32)
        partial = local(expert_kernel, shape, sent, other_core(sent), in_high, in_low, out_high, out_low)
        partial = partial + other_core(partial)
        first, second = partial[:half], partial[half:]
        own = pick(core, second, first) + sum(plane(pick(core, first, second)))
        arrived = [along_expert(own, k) for k in order]
        own_near = other_core(own)
        shape = pltpu.VMEM((n_expert - 1, half, rows, LANES), f32)
        others = local(stack_kernel, shape, combine, *arrived, own_near)

        def mix(near, own, others, *out):
            return pl.pallas_call(
                functools.partial(mix_kernel, near),
                out_shape=jax.ShapeDtypeStruct((count, width), f32),
                in_specs=[VMEM, VMEM, VMEM] + [HBM] * len(out),
                out_specs=HBM,
                scratch_shapes=[
                    pltpu.VMEM((slots, half * LANES), f32),
                    pltpu.VMEM((count, half * LANES), f32),
                    pltpu.SemaphoreType.DMA((4,)),
                ],
                input_output_aliases={3: 0} if out else {},
                compiler_params=params,
            )(combine, own, others, *out)

        mixed = mix(True, own_near, others)
        return mix(False, own, other_core(others), mixed)

    return jax.shard_map(
        body,
        mesh=mesh,
        in_specs=(P(AXES, None), P(), P("expert", ("seq", "fsdp"), None), P("expert", ("seq", "fsdp"), None)),
        out_specs=P(AXES, None),
        check_vma=False,
    )
```

```python
import functools

import jax
import jax.numpy as jnp
from jax import lax
from jax.experimental import pallas as pl
from jax.experimental.pallas import tpu as pltpu
from jax.sharding import PartitionSpec as P

SLOTS = 4
LANES = 128
AXES = ("expert", "seq", "fsdp")
VMEM = pl.BlockSpec(memory_space=pltpu.VMEM)
HBM = pl.BlockSpec(memory_space=pltpu.HBM)


def pieces(value, count):
    out = []
    for _ in range(count):
        part = value.astype(jnp.bfloat16)
        out.append(part)
        value = value - part.astype(jnp.float32)
    return out


def stacked(value):
    high, low = pieces(value, 2)
    return jnp.concatenate([high.astype(jnp.float32), low.astype(jnp.float32)], axis=0).astype(jnp.bfloat16)


def mm(left, right, contract=((1,), (0,))):
    return lax.dot_general(left, right, (contract, ((), ())), preferred_element_type=jnp.float32)


def pick(core, when_zero, when_one):
    return jnp.where(core == 0, when_zero, when_one)


def join(parts):
    top = functools.reduce(jnp.maximum, [p[-1] for p in parts])
    total = sum(p[:-1] * jnp.exp(p[-1] - top)[None] for p in parts)
    return jnp.concatenate([total, top[None]], axis=0)


def dispatch_kernel(chunks, tokens_hbm, params_hbm, w_in_hbm, logits_ref, mine_ref, theirs_ref, w_in_ref,
                    tokens_ref, params_ref, sums_ref, sems):
    core, expert = lax.axis_index("seq") % 2, lax.axis_index("expert")
    groups, tiles, rows, _ = mine_ref.shape
    half = tiles - 2
    slots, width = params_hbm.shape
    copies = [pltpu.make_async_copy(params_hbm, params_ref, sems.at[0])]
    for start, stop in chunks:
        own = pl.ds(start, stop - start)
        copies.append(pltpu.make_async_copy(tokens_hbm.at[own], tokens_ref.at[own], sems.at[len(copies)]))
    copies.append(pltpu.make_async_copy(w_in_hbm, w_in_ref, sems.at[len(copies)]))
    for copy in copies:
        copy.start()
    copies[0].wait()
    params = jnp.concatenate(pieces(params_ref[...], 3), axis=0)
    highs, lows, logits = [], [], []
    nt = ((1,), (1,))
    for (start, stop), copy in zip(chunks, copies[1:]):
        copy.wait()
        high, low, rest = pieces(tokens_ref[start:stop], 3)
        highs.append(high)
        lows.append(low)
        a = mm(params, high, nt)
        b = mm(params[:2 * slots], low, nt)
        c = mm(params[:slots], rest, nt)
        small = a[2 * slots:] + b[slots:] + c
        logits.append((small + (a[slots:2 * slots] + b[:slots])) + a[:slots])
    logits = jnp.concatenate(logits, axis=1)
    logits_ref[...] = logits
    peak = jnp.max(logits, axis=1, keepdims=True)
    weights = jnp.exp(logits - peak)
    mass = jnp.sum(weights, axis=1, keepdims=True)
    weight_high, weight_low = pieces(weights, 2)
    high = mm(jnp.concatenate([weight_high, weight_low], axis=0), jnp.concatenate(highs, axis=0))
    low = mm(weight_high, jnp.concatenate(lows, axis=0))
    sums_ref[:, :width] = high[:slots] + (high[slots:] + low)
    sums_ref[:, width:width + LANES] = jnp.broadcast_to(mass, (slots, LANES))
    sums_ref[:, width + LANES:] = jnp.broadcast_to(peak, (slots, LANES))
    for k in range(groups):
        own = pl.ds(pl.multiple_of((expert ^ k) * rows, rows), rows)
        sides = (core, 1 - core) if k else (1 - core, core)
        for ref, side in zip((mine_ref, theirs_ref), sides):
            for t in range(half):
                place = pl.ds(pl.multiple_of((side * half + t) * LANES, LANES), LANES)
                ref[k, t] = sums_ref[own, place]
            for t in range(2):
                ref[k, half + t] = sums_ref[own, width + t * LANES:width + (t + 1) * LANES]
    copies[-1].wait()


def chip_kernel(mine_ref, theirs_ref, *outs):
    for k, out_ref in enumerate(outs):
        out_ref[...] = join([mine_ref[k], theirs_ref[k]])


def split_out_kernel(_, w_hbm, high_ref, low_ref, flag_ref, w_ref, sems):
    experts, units, _ = w_hbm.shape
    parts = sems.shape[0] // experts
    count = units // parts
    copies = []
    for e in range(experts):
        for i in range(parts):
            own = pl.ds(i * count, count)
            copies.append(pltpu.make_async_copy(w_hbm.at[e, own], w_ref.at[e, own], sems.at[len(copies)]))
            copies[-1].start()
    for e in range(experts):
        for i in range(parts):
            copies[e * parts + i].wait()
            start = e * units + i * count
            own = slice(start, start + count)
            high_ref[own], low_ref[own] = pieces(w_ref[e, i * count:(i + 1) * count], 2)
    flag_ref[...] = jnp.zeros_like(flag_ref)


def split_in_kernel(_, w_ref, high_ref, low_ref, flag_ref):
    experts, units, width = w_ref.shape
    high, low = pieces(w_ref[...].reshape(experts * units, width), 2)
    high_ref[...] = high.T
    low_ref[...] = low.T
    flag_ref[...] = jnp.zeros_like(flag_ref)


def total_kernel(own_ref, *refs):
    *others, _, out_ref = refs
    out_ref[...] = join([own_ref[...]] + [r[...] for r in others])


def plane_kernel(own_ref, *refs):
    *others, _, out_ref = refs
    out_ref[0] = join([r[...] for r in others])
    out_ref[1] = own_ref[...]


def halves_kernel(mine_ref, theirs_ref, keep_ref, send_ref):
    core = lax.axis_index("seq") % 2
    half = keep_ref.shape[0]
    for ref, side in ((send_ref, core), (keep_ref, 1 - core)):
        own = pl.ds(side * half, half)
        ref[...] = mine_ref[own] + theirs_ref[own]


def add_kernel(own_ref, *refs):
    *others, out_ref = refs
    out_ref[...] = own_ref[...] + sum(r[...] for r in others)


def stack_kernel(*refs):
    _, *others, _, out_ref = refs
    for k, r in enumerate(reversed(others)):
        out_ref[k] = r[...]


def combine_kernel(logits_ref, out_ref):
    logits = logits_ref[...]
    top = jnp.max(logits, axis=0, keepdims=True)
    powers = jnp.exp(logits - top)
    combine = (powers / jnp.sum(powers, axis=0, keepdims=True)).T
    high, low = pieces(combine, 2)
    out_ref[...] = jnp.concatenate([high, low, high], axis=1)


def expert_kernel(sent_ref, got_ref, in_high_ref, in_low_ref, out_high_ref, out_low_ref, out_ref):
    core = lax.axis_index("seq") % 2
    tiles, rows, _ = out_ref.shape
    half = tiles // 2
    experts = rows // SLOTS
    units = in_high_ref.shape[1] // experts
    near = join([sent_ref[0], got_ref[1]])
    far = join([sent_ref[1], got_ref[0]])
    near = [near[t] / near[half] for t in range(half)]
    far = [far[t] / far[half] for t in range(half)]
    first = [pick(core, a, b) for a, b in zip(near, far)]
    second = [pick(core, b, a) for a, b in zip(near, far)]
    inputs = stacked(jnp.concatenate(first + second, axis=1))
    large = mm(inputs, in_high_ref[...])
    small = mm(inputs, in_low_ref[...])
    value = large[:rows] + (large[rows:] + small[:rows])
    value = value * (1.0 + lax.erf(value * (0.5 ** 0.5))) * 0.5
    slot = lax.broadcasted_iota(jnp.int32, value.shape, 0)
    unit = lax.broadcasted_iota(jnp.int32, value.shape, 1)
    keep = None
    for e in range(experts):
        inside = (slot // SLOTS == e) & (unit >= e * units) & (unit < (e + 1) * units)
        keep = inside if keep is None else keep | inside
    hidden = stacked(jnp.where(keep, value, 0.0))
    large = mm(hidden, out_high_ref[...])
    small = mm(hidden, out_low_ref[...])
    out = large[:rows] + (large[rows:] + small[:rows])
    for t in range(tiles):
        out_ref[t] = out[:, t * LANES:(t + 1) * LANES]


def mix_kernel(near, combine_ref, own_ref, others_ref, *refs):
    out_hbm, slots_ref, out_ref, sems = refs[-4:]
    core, expert = lax.axis_index("seq") % 2, lax.axis_index("expert")
    half, rows, _ = own_ref.shape
    groups = others_ref.shape[0] + 1
    for k in range(groups):
        place = pl.ds(pl.multiple_of((expert ^ k) * rows, rows), rows)
        for t in range(half):
            slots_ref[place, t * LANES:(t + 1) * LANES] = others_ref[k - 1, t] if k else own_ref[t]
    high, low = pieces(slots_ref[...], 2)
    slots = jnp.concatenate([high, high, low], axis=0)
    side = core if near else 1 - core
    columns = pl.ds(pl.multiple_of(side * (half * LANES), LANES), half * LANES)
    count = combine_ref.shape[0]
    step = pl.cdiv(count, 16 * sems.shape[0]) * 16
    copies = []
    for i, start in enumerate(range(0, count, step)):
        size = min(step, count - start)
        out_ref[start:start + size] = mm(combine_ref[start:start + size], slots)
        place = pl.ds(start, size)
        copies.append(pltpu.make_async_copy(out_ref.at[place], out_hbm.at[place, columns], sems.at[i]))
        copies[i].start()
    for copy in copies:
        copy.wait()


def solution(mesh):
    n_expert, n_seq, n_fsdp = (mesh.shape[a] for a in AXES)
    n_x = n_seq // 2

    def permute(value, target):
        pairs = []
        for e in range(n_expert):
            for s in range(n_seq):
                for f in range(n_fsdp):
                    te, tx, tc, tf = target(e, s // 2, s % 2, f)
                    pairs.append(((e * n_seq + s) * n_fsdp + f, (te * n_seq + tx * 2 + tc) * n_fsdp + tf))
        return lax.ppermute(value, AXES, pairs)

    def other_core(value):
        return permute(value, lambda e, x, c, f: (e, x, 1 - c, f))

    def along_expert(value, k):
        return permute(value, lambda e, x, c, f: (e ^ k, x, 1 - c, f))

    def plane(value):
        return [
            permute(value, lambda e, x, c, f, dx=dx, df=df: (e, (x + dx) % n_x, 1 - c, (f + df) % n_fsdp))
            for dx in range(n_x)[::-1] for df in range(n_fsdp)[::-1] if dx or df
        ]

    def body(tokens, slot_params, w_in, w_out):
        count, width = tokens.shape
        slots = slot_params.shape[1]
        rows = w_in.shape[0] * SLOTS
        half = width // LANES // 2
        f32 = jnp.float32
        params = pltpu.CompilerParams(vmem_limit_bytes=24 * 1024 * 1024)
        core = lax.axis_index("seq") % 2
        chunks = [(0, count)]
        in_hbm = lambda value: pltpu.with_memory_space_constraint(value, pltpu.HBM)
        shape = pltpu.VMEM((n_expert, half + 2, rows, LANES), f32)
        logits, mine, theirs, w_in = pl.pallas_call(
            functools.partial(dispatch_kernel, chunks),
            out_shape=(pltpu.VMEM((slots, count), f32), shape, shape, pltpu.VMEM(w_in.shape, f32)),
            in_specs=[HBM, HBM, HBM],
            out_specs=(VMEM,) * 4,
            scratch_shapes=[
                pltpu.VMEM((count, width), f32),
                pltpu.VMEM((slots, width), f32),
                pltpu.VMEM((slots, width + 2 * LANES), f32),
                pltpu.SemaphoreType.DMA((len(chunks) + 2,)),
            ],
            compiler_params=params,
        )(in_hbm(tokens), in_hbm(slot_params.T), in_hbm(w_in))
        combine = pl.pallas_call(
            combine_kernel,
            out_shape=jax.ShapeDtypeStruct((count, 3 * slots), jnp.bfloat16),
            in_specs=[VMEM],
            out_specs=VMEM,
            compiler_params=params,
        )(logits)

        chip = pl.pallas_call(
            chip_kernel,
            out_shape=(pltpu.VMEM((half + 2, rows, LANES), f32),) * n_expert,
            in_specs=[VMEM, VMEM],
            out_specs=(VMEM,) * n_expert,
            compiler_params=params,
        )(mine, other_core(theirs))
        order = list(range(n_expert - 1, 0, -1))
        flag = pltpu.VMEM((8, LANES), f32)
        experts, units, _ = w_in.shape
        cost = pl.CostEstimate(flops=8 * w_in.size, bytes_accessed=8 * w_in.size, transcendentals=0)

        def local(kernel, out, *args):
            return pl.pallas_call(
                kernel,
                out_shape=out,
                in_specs=[VMEM] * len(args),
                out_specs=jax.tree.map(lambda _: VMEM, out),
                compiler_params=params,
            )(*args)

        part = pltpu.VMEM((experts * units, width), jnp.bfloat16)
        parts = 4 if units % 64 == 0 else 1
        out_high, out_low, ready = pl.pallas_call(
            split_out_kernel,
            out_shape=(part, part, flag),
            in_specs=[VMEM, HBM],
            out_specs=(VMEM,) * 3,
            scratch_shapes=[pltpu.VMEM(w_out.shape, f32), pltpu.SemaphoreType.DMA((experts * parts,))],
            cost_estimate=cost,
            compiler_params=params,
        )(chip[0], in_hbm(w_out))
        shape = pltpu.VMEM((half + 2, rows, LANES), f32)
        total = local(total_kernel, shape, chip[0], *[along_expert(chip[k], k) for k in order], ready)
        part = pltpu.VMEM((width, experts * units), jnp.bfloat16)
        in_high, in_low, ready = pl.pallas_call(
            split_in_kernel,
            out_shape=(part, part, flag),
            in_specs=[VMEM, VMEM],
            out_specs=(VMEM,) * 3,
            cost_estimate=cost,
            compiler_params=params,
        )(total, w_in)
        shape = pltpu.VMEM((2, half + 2, rows, LANES), f32)
        sent = local(plane_kernel, shape, total, *plane(total), ready)
        shape = pltpu.VMEM((2 * half, rows, LANES), f32)
        partial = local(expert_kernel, shape, sent, other_core(sent), in_high, in_low, out_high, out_low)
        shape = pltpu.VMEM((half, rows, LANES), f32)
        keep, send = local(halves_kernel, (shape, shape), partial, other_core(partial))
        around = plane(send)
        own = local(add_kernel, shape, keep, *around[-1:], *around[:-1])
        arrived = [along_expert(own, k) for k in order]
        own_near = other_core(own)
        shape = pltpu.VMEM((n_expert - 1, half, rows, LANES), f32)
        others = local(stack_kernel, shape, combine, *arrived, own_near)

        def mix(near, own, others, *out):
            return pl.pallas_call(
                functools.partial(mix_kernel, near),
                out_shape=jax.ShapeDtypeStruct((count, width), f32),
                in_specs=[VMEM, VMEM, VMEM] + [HBM] * len(out),
                out_specs=HBM,
                scratch_shapes=[
                    pltpu.VMEM((slots, half * LANES), f32),
                    pltpu.VMEM((count, half * LANES), f32),
                    pltpu.SemaphoreType.DMA((4,)),
                ],
                input_output_aliases={3: 0} if out else {},
                compiler_params=params,
            )(combine, own, others, *out)

        mixed = mix(True, own_near, others)
        return mix(False, own, other_core(others), mixed)

    return jax.shard_map(
        body,
        mesh=mesh,
        in_specs=(P(AXES, None), P(), P("expert", ("seq", "fsdp"), None), P("expert", ("seq", "fsdp"), None)),
        out_specs=P(AXES, None),
        check_vma=False,
    )
```

```python
import functools

import jax
import jax.numpy as jnp
from jax import lax
from jax.experimental import pallas as pl
from jax.experimental.pallas import tpu as pltpu
from jax.sharding import PartitionSpec as P

SLOTS = 4
LANES = 128
AXES = ("expert", "seq", "fsdp")
VMEM = pl.BlockSpec(memory_space=pltpu.VMEM)
HBM = pl.BlockSpec(memory_space=pltpu.HBM)


def pieces(value, count):
    out = []
    for _ in range(count):
        part = value.astype(jnp.bfloat16)
        out.append(part)
        value = value - part.astype(jnp.float32)
    return out


def stacked(value):
    high, low = pieces(value, 2)
    return jnp.concatenate([high.astype(jnp.float32), low.astype(jnp.float32)], axis=0).astype(jnp.bfloat16)


def mm(left, right, contract=((1,), (0,))):
    return lax.dot_general(left, right, (contract, ((), ())), preferred_element_type=jnp.float32)


def pick(core, when_zero, when_one):
    return jnp.where(core == 0, when_zero, when_one)


def join(parts):
    top = functools.reduce(jnp.maximum, [p[-1] for p in parts])
    total = sum(p[:-1] * jnp.exp(p[-1] - top)[None] for p in parts)
    return jnp.concatenate([total, top[None]], axis=0)


def dispatch_kernel(chunks, tokens_hbm, params_hbm, w_in_hbm, logits_ref, mine_ref, theirs_ref, w_in_ref,
                    tokens_ref, params_ref, sums_ref, sems):
    core, expert = lax.axis_index("seq") % 2, lax.axis_index("expert")
    groups, tiles, rows, _ = mine_ref.shape
    half = tiles - 2
    slots, width = params_hbm.shape
    copies = [pltpu.make_async_copy(params_hbm, params_ref, sems.at[0])]
    for start, stop in chunks:
        own = pl.ds(start, stop - start)
        copies.append(pltpu.make_async_copy(tokens_hbm.at[own], tokens_ref.at[own], sems.at[len(copies)]))
    copies.append(pltpu.make_async_copy(w_in_hbm, w_in_ref, sems.at[len(copies)]))
    for copy in copies:
        copy.start()
    copies[0].wait()
    params = jnp.concatenate(pieces(params_ref[...], 3), axis=0)
    for copy in copies[1:-1]:
        copy.wait()
    token_high, token_low, rest = pieces(tokens_ref[...], 3)
    nt = ((1,), (1,))
    a = mm(params, token_high, nt)
    b = mm(params[:2 * slots], token_low, nt)
    c = mm(params[:slots], rest, nt)
    small = a[2 * slots:] + b[slots:] + c
    logits = (small + (a[slots:2 * slots] + b[:slots])) + a[:slots]
    logits_ref[...] = logits
    peak = jnp.max(logits, axis=1, keepdims=True)
    weights = jnp.exp(logits - peak)
    mass = jnp.sum(weights, axis=1, keepdims=True)
    weight_high, weight_low = pieces(weights, 2)
    high = mm(jnp.concatenate([weight_high, weight_low], axis=0), token_high)
    low = mm(weight_high, token_low)
    sums_ref[:, :width] = high[:slots] + (high[slots:] + low)
    sums_ref[:, width:width + LANES] = jnp.broadcast_to(mass, (slots, LANES))
    sums_ref[:, width + LANES:] = jnp.broadcast_to(peak, (slots, LANES))
    for k in range(groups):
        own = pl.ds(pl.multiple_of((expert ^ k) * rows, rows), rows)
        sides = (core, 1 - core) if k else (1 - core, core)
        for ref, side in zip((mine_ref, theirs_ref), sides):
            for t in range(half):
                place = pl.ds(pl.multiple_of((side * half + t) * LANES, LANES), LANES)
                ref[k, t] = sums_ref[own, place]
            for t in range(2):
                ref[k, half + t] = sums_ref[own, width + t * LANES:width + (t + 1) * LANES]
    copies[-1].wait()


def chip_kernel(mine_ref, theirs_ref, *outs):
    for k, out_ref in enumerate(outs):
        out_ref[...] = join([mine_ref[k], theirs_ref[k]])


def split_out_kernel(_, w_hbm, high_ref, low_ref, flag_ref, w_ref, sems):
    experts, units, _ = w_hbm.shape
    parts = sems.shape[0] // experts
    count = units // parts
    copies = []
    for e in range(experts):
        for i in range(parts):
            own = pl.ds(i * count, count)
            copies.append(pltpu.make_async_copy(w_hbm.at[e, own], w_ref.at[e, own], sems.at[len(copies)]))
            copies[-1].start()
    for e in range(experts):
        for i in range(parts):
            copies[e * parts + i].wait()
            start = e * units + i * count
            own = slice(start, start + count)
            high_ref[own], low_ref[own] = pieces(w_ref[e, i * count:(i + 1) * count], 2)
    flag_ref[...] = jnp.zeros_like(flag_ref)


def split_in_kernel(_, w_ref, high_ref, low_ref, flag_ref):
    experts, units, width = w_ref.shape
    high, low = pieces(w_ref[...].reshape(experts * units, width), 2)
    high_ref[...] = high.T
    low_ref[...] = low.T
    flag_ref[...] = jnp.zeros_like(flag_ref)


def total_kernel(own_ref, *refs):
    *others, _, out_ref = refs
    out_ref[...] = join([own_ref[...]] + [r[...] for r in others])


def plane_kernel(own_ref, *refs):
    *others, _, out_ref = refs
    out_ref[0] = join([r[...] for r in others])
    out_ref[1] = own_ref[...]


def halves_kernel(mine_ref, theirs_ref, keep_ref, send_ref):
    core = lax.axis_index("seq") % 2
    half = keep_ref.shape[0]
    for ref, side in ((send_ref, core), (keep_ref, 1 - core)):
        own = pl.ds(side * half, half)
        ref[...] = mine_ref[own] + theirs_ref[own]


def add_kernel(own_ref, *refs):
    *others, out_ref = refs
    out_ref[...] = own_ref[...] + sum(r[...] for r in others)


def stack_kernel(*refs):
    _, *others, _, out_ref = refs
    for k, r in enumerate(others):
        out_ref[k] = r[...]


def combine_kernel(logits_ref, out_ref):
    logits = logits_ref[...]
    top = jnp.max(logits, axis=0, keepdims=True)
    powers = jnp.exp(logits - top)
    combine = (powers / jnp.sum(powers, axis=0, keepdims=True)).T
    high, low = pieces(combine, 2)
    out_ref[...] = jnp.concatenate([high, low, high], axis=1)


def expert_kernel(sent_ref, got_ref, in_high_ref, in_low_ref, out_high_ref, out_low_ref, out_ref):
    core = lax.axis_index("seq") % 2
    tiles, rows, _ = out_ref.shape
    half = tiles // 2
    experts = rows // SLOTS
    units = in_high_ref.shape[1] // experts
    near = join([sent_ref[0], got_ref[1]])
    far = join([sent_ref[1], got_ref[0]])
    near = [near[t] / near[half] for t in range(half)]
    far = [far[t] / far[half] for t in range(half)]
    first = [pick(core, a, b) for a, b in zip(near, far)]
    second = [pick(core, b, a) for a, b in zip(near, far)]
    inputs = stacked(jnp.concatenate(first + second, axis=1))
    large = mm(inputs, in_high_ref[...])
    small = mm(inputs, in_low_ref[...])
    value = large[:rows] + (large[rows:] + small[:rows])
    value = value * (1.0 + lax.erf(value * (0.5 ** 0.5))) * 0.5
    slot = lax.broadcasted_iota(jnp.int32, value.shape, 0)
    unit = lax.broadcasted_iota(jnp.int32, value.shape, 1)
    keep = None
    for e in range(experts):
        inside = (slot // SLOTS == e) & (unit >= e * units) & (unit < (e + 1) * units)
        keep = inside if keep is None else keep | inside
    hidden = stacked(jnp.where(keep, value, 0.0))
    large = mm(hidden, out_high_ref[...])
    small = mm(hidden, out_low_ref[...])
    out = large[:rows] + (large[rows:] + small[:rows])
    for t in range(tiles):
        out_ref[t] = out[:, t * LANES:(t + 1) * LANES]


def mix_kernel(near, combine_ref, own_ref, others_ref, *refs):
    out_hbm, slots_ref, out_ref, sems = refs[-4:]
    core, expert = lax.axis_index("seq") % 2, lax.axis_index("expert")
    half, rows, _ = own_ref.shape
    groups = others_ref.shape[0] + 1
    for k in range(groups):
        place = pl.ds(pl.multiple_of(lax.rem(expert - k + groups, groups) * rows, rows), rows)
        for t in range(half):
            slots_ref[place, t * LANES:(t + 1) * LANES] = others_ref[k - 1, t] if k else own_ref[t]
    high, low = pieces(slots_ref[...], 2)
    slots = jnp.concatenate([high, high, low], axis=0)
    side = core if near else 1 - core
    columns = pl.ds(pl.multiple_of(side * (half * LANES), LANES), half * LANES)
    count = combine_ref.shape[0]
    step = pl.cdiv(count, 16 * sems.shape[0]) * 16
    copies = []
    for i, start in enumerate(range(0, count, step)):
        size = min(step, count - start)
        out_ref[start:start + size] = mm(combine_ref[start:start + size], slots)
        place = pl.ds(start, size)
        copies.append(pltpu.make_async_copy(out_ref.at[place], out_hbm.at[place, columns], sems.at[i]))
        copies[i].start()
    for copy in copies:
        copy.wait()


def solution(mesh):
    n_expert, n_seq, n_fsdp = (mesh.shape[a] for a in AXES)
    n_x = n_seq // 2

    def permute(value, target):
        pairs = []
        for e in range(n_expert):
            for s in range(n_seq):
                for f in range(n_fsdp):
                    te, tx, tc, tf = target(e, s // 2, s % 2, f)
                    pairs.append(((e * n_seq + s) * n_fsdp + f, (te * n_seq + tx * 2 + tc) * n_fsdp + tf))
        return lax.ppermute(value, AXES, pairs)

    def other_core(value):
        return permute(value, lambda e, x, c, f: (e, x, 1 - c, f))

    def along_expert(value, k):
        return permute(value, lambda e, x, c, f: (e ^ k, x, 1 - c, f))

    def around_expert(value, k):
        return permute(value, lambda e, x, c, f: ((e + k) % n_expert, x, 1 - c, f))

    def plane(value):
        return [
            permute(value, lambda e, x, c, f, dx=dx, df=df: (e, (x + dx) % n_x, 1 - c, (f + df) % n_fsdp))
            for dx in range(n_x)[::-1] for df in range(n_fsdp)[::-1] if dx or df
        ]

    def body(tokens, slot_params, w_in, w_out):
        count, width = tokens.shape
        slots = slot_params.shape[1]
        rows = w_in.shape[0] * SLOTS
        half = width // LANES // 2
        f32 = jnp.float32
        params = pltpu.CompilerParams(vmem_limit_bytes=24 * 1024 * 1024)
        core = lax.axis_index("seq") % 2
        step = count // 4 if count % 32 == 0 else count
        chunks = [(i, i + step) for i in range(0, count, step)]
        in_hbm = lambda value: pltpu.with_memory_space_constraint(value, pltpu.HBM)
        shape = pltpu.VMEM((n_expert, half + 2, rows, LANES), f32)
        logits, mine, theirs, w_in = pl.pallas_call(
            functools.partial(dispatch_kernel, chunks),
            out_shape=(pltpu.VMEM((slots, count), f32), shape, shape, pltpu.VMEM(w_in.shape, f32)),
            in_specs=[HBM, HBM, HBM],
            out_specs=(VMEM,) * 4,
            scratch_shapes=[
                pltpu.VMEM((count, width), f32),
                pltpu.VMEM((slots, width), f32),
                pltpu.VMEM((slots, width + 2 * LANES), f32),
                pltpu.SemaphoreType.DMA((len(chunks) + 2,)),
            ],
            compiler_params=params,
        )(in_hbm(tokens), in_hbm(slot_params.T), in_hbm(w_in))
        combine = pl.pallas_call(
            combine_kernel,
            out_shape=jax.ShapeDtypeStruct((count, 3 * slots), jnp.bfloat16),
            in_specs=[VMEM],
            out_specs=VMEM,
            compiler_params=params,
        )(logits)

        chip = pl.pallas_call(
            chip_kernel,
            out_shape=(pltpu.VMEM((half + 2, rows, LANES), f32),) * n_expert,
            in_specs=[VMEM, VMEM],
            out_specs=(VMEM,) * n_expert,
            compiler_params=params,
        )(mine, other_core(theirs))
        order = list(range(n_expert - 1, 0, -1))
        flag = pltpu.VMEM((8, LANES), f32)
        experts, units, _ = w_in.shape
        cost = pl.CostEstimate(flops=8 * w_in.size, bytes_accessed=8 * w_in.size, transcendentals=0)

        def local(kernel, out, *args):
            return pl.pallas_call(
                kernel,
                out_shape=out,
                in_specs=[VMEM] * len(args),
                out_specs=jax.tree.map(lambda _: VMEM, out),
                compiler_params=params,
            )(*args)

        part = pltpu.VMEM((experts * units, width), jnp.bfloat16)
        parts = 4 if units % 64 == 0 else 1
        out_high, out_low, ready = pl.pallas_call(
            split_out_kernel,
            out_shape=(part, part, flag),
            in_specs=[VMEM, HBM],
            out_specs=(VMEM,) * 3,
            scratch_shapes=[pltpu.VMEM(w_out.shape, f32), pltpu.SemaphoreType.DMA((experts * parts,))],
            cost_estimate=cost,
            compiler_params=params,
        )(chip[0], in_hbm(w_out))
        shape = pltpu.VMEM((half + 2, rows, LANES), f32)
        total = local(total_kernel, shape, chip[0], *[along_expert(chip[k], k) for k in order], ready)
        part = pltpu.VMEM((width, experts * units), jnp.bfloat16)
        in_high, in_low, ready = pl.pallas_call(
            split_in_kernel,
            out_shape=(part, part, flag),
            in_specs=[VMEM, VMEM],
            out_specs=(VMEM,) * 3,
            cost_estimate=cost,
            compiler_params=params,
        )(total, w_in)
        shape = pltpu.VMEM((2, half + 2, rows, LANES), f32)
        sent = local(plane_kernel, shape, total, *plane(total), ready)
        shape = pltpu.VMEM((2 * half, rows, LANES), f32)
        partial = local(expert_kernel, shape, sent, other_core(sent), in_high, in_low, out_high, out_low)
        shape = pltpu.VMEM((half, rows, LANES), f32)
        keep, send = local(halves_kernel, (shape, shape), partial, other_core(partial))
        around = plane(send)
        own = local(add_kernel, shape, keep, *around[-1:], *around[:-1])
        arrived = [around_expert(own, k) for k in range(1, n_expert)]
        own_near = other_core(own)
        shape = pltpu.VMEM((n_expert - 1, half, rows, LANES), f32)
        others = local(stack_kernel, shape, combine, *arrived, own_near)

        def mix(near, own, others, *out):
            return pl.pallas_call(
                functools.partial(mix_kernel, near),
                out_shape=jax.ShapeDtypeStruct((count, width), f32),
                in_specs=[VMEM, VMEM, VMEM] + [HBM] * len(out),
                out_specs=HBM,
                scratch_shapes=[
                    pltpu.VMEM((slots, half * LANES), f32),
                    pltpu.VMEM((count, half * LANES), f32),
                    pltpu.SemaphoreType.DMA((4,)),
                ],
                input_output_aliases={3: 0} if out else {},
                compiler_params=params,
            )(combine, own, others, *out)

        mixed = mix(True, own_near, others)
        return mix(False, own, other_core(others), mixed)

    return jax.shard_map(
        body,
        mesh=mesh,
        in_specs=(P(AXES, None), P(), P("expert", ("seq", "fsdp"), None), P("expert", ("seq", "fsdp"), None)),
        out_specs=P(AXES, None),
        check_vma=False,
    )
```

```python
import functools

import jax
import jax.numpy as jnp
from jax import lax
from jax.experimental import pallas as pl
from jax.experimental.pallas import tpu as pltpu
from jax.sharding import PartitionSpec as P

SLOTS = 4
LANES = 128
AXES = ("expert", "seq", "fsdp")
VMEM = pl.BlockSpec(memory_space=pltpu.VMEM)
HBM = pl.BlockSpec(memory_space=pltpu.HBM)


def pieces(value, count):
    out = []
    for _ in range(count):
        part = value.astype(jnp.bfloat16)
        out.append(part)
        value = value - part.astype(jnp.float32)
    return out


def stacked(value):
    high, low = pieces(value, 2)
    return jnp.concatenate([high.astype(jnp.float32), low.astype(jnp.float32)], axis=0).astype(jnp.bfloat16)


def mm(left, right, contract=((1,), (0,))):
    return lax.dot_general(left, right, (contract, ((), ())), preferred_element_type=jnp.float32)


def pick(core, when_zero, when_one):
    return jnp.where(core == 0, when_zero, when_one)


def ring_step(e, k, n, where=lambda c, a, b: a if c else b):
    place = where(e % 2 == 1, (e + 1) // 2, n - e // 2) + k
    place = where(place >= n, place - n, place)
    return where(place == 0, 0, where(place <= n // 2, 2 * place - 1, 2 * (n - place)))


def join(parts):
    top = functools.reduce(jnp.maximum, [p[-1] for p in parts])
    total = sum(p[:-1] * jnp.exp(p[-1] - top)[None] for p in parts)
    return jnp.concatenate([total, top[None]], axis=0)


def dispatch_kernel(chunks, tokens_hbm, params_hbm, w_in_hbm, logits_ref, mine_ref, theirs_ref, w_in_ref,
                    tokens_ref, params_ref, sums_ref, sems):
    core, expert = lax.axis_index("seq") % 2, lax.axis_index("expert")
    groups, tiles, rows, _ = mine_ref.shape
    half = tiles - 2
    slots, width = params_hbm.shape
    copies = [pltpu.make_async_copy(params_hbm, params_ref, sems.at[0])]
    for start, stop in chunks:
        own = pl.ds(start, stop - start)
        copies.append(pltpu.make_async_copy(tokens_hbm.at[own], tokens_ref.at[own], sems.at[len(copies)]))
    copies.append(pltpu.make_async_copy(w_in_hbm, w_in_ref, sems.at[len(copies)]))
    for copy in copies:
        copy.start()
    copies[0].wait()
    params = jnp.concatenate(pieces(params_ref[...], 3), axis=0)
    for copy in copies[1:-1]:
        copy.wait()
    token_high, token_low, rest = pieces(tokens_ref[...], 3)
    nt = ((1,), (1,))
    a = mm(params, token_high, nt)
    b = mm(params[:2 * slots], token_low, nt)
    c = mm(params[:slots], rest, nt)
    small = a[2 * slots:] + b[slots:] + c
    logits = (small + (a[slots:2 * slots] + b[:slots])) + a[:slots]
    logits_ref[...] = logits
    peak = jnp.max(logits, axis=1, keepdims=True)
    weights = jnp.exp(logits - peak)
    mass = jnp.sum(weights, axis=1, keepdims=True)
    weight_high, weight_low = pieces(weights, 2)
    high = mm(jnp.concatenate([weight_high, weight_low], axis=0), token_high)
    low = mm(weight_high, token_low)
    sums_ref[:, :width] = high[:slots] + (high[slots:] + low)
    sums_ref[:, width:width + LANES] = jnp.broadcast_to(mass, (slots, LANES))
    sums_ref[:, width + LANES:] = jnp.broadcast_to(peak, (slots, LANES))
    for k in range(groups):
        target = ring_step(expert, k, groups, jnp.where)
        own = pl.ds(pl.multiple_of(target * rows, rows), rows)
        sides = (core, 1 - core) if k else (1 - core, core)
        for ref, side in zip((mine_ref, theirs_ref), sides):
            for t in range(half):
                place = pl.ds(pl.multiple_of((side * half + t) * LANES, LANES), LANES)
                ref[k, t] = sums_ref[own, place]
            for t in range(2):
                ref[k, half + t] = sums_ref[own, width + t * LANES:width + (t + 1) * LANES]
    copies[-1].wait()


def chip_kernel(mine_ref, theirs_ref, *outs):
    for k, out_ref in enumerate(outs):
        out_ref[...] = join([mine_ref[k], theirs_ref[k]])


def split_out_kernel(_, w_hbm, high_ref, low_ref, flag_ref, w_ref, sems):
    experts, units, _ = w_hbm.shape
    parts = sems.shape[0] // experts
    count = units // parts
    copies = []
    for e in range(experts):
        for i in range(parts):
            own = pl.ds(i * count, count)
            copies.append(pltpu.make_async_copy(w_hbm.at[e, own], w_ref.at[e, own], sems.at[len(copies)]))
            copies[-1].start()
    for e in range(experts):
        for i in range(parts):
            copies[e * parts + i].wait()
            start = e * units + i * count
            own = slice(start, start + count)
            high_ref[own], low_ref[own] = pieces(w_ref[e, i * count:(i + 1) * count], 2)
    flag_ref[...] = jnp.zeros_like(flag_ref)


def split_in_kernel(_, w_ref, high_ref, low_ref, flag_ref):
    experts, units, width = w_ref.shape
    high, low = pieces(w_ref[...].reshape(experts * units, width), 2)
    high_ref[...] = high.T
    low_ref[...] = low.T
    flag_ref[...] = jnp.zeros_like(flag_ref)


def total_kernel(own_ref, *refs):
    *others, _, out_ref = refs
    out_ref[...] = join([own_ref[...]] + [r[...] for r in others])


def plane_kernel(own_ref, *refs):
    *others, _, out_ref = refs
    out_ref[0] = join([r[...] for r in others])
    out_ref[1] = own_ref[...]


def halves_kernel(mine_ref, theirs_ref, keep_ref, send_ref):
    core = lax.axis_index("seq") % 2
    half = keep_ref.shape[0]
    for ref, side in ((send_ref, core), (keep_ref, 1 - core)):
        own = pl.ds(side * half, half)
        ref[...] = mine_ref[own] + theirs_ref[own]


def add_kernel(own_ref, *refs):
    *others, out_ref = refs
    out_ref[...] = own_ref[...] + sum(r[...] for r in others)


def stack_kernel(*refs):
    _, *others, _, out_ref = refs
    for k, r in enumerate(others):
        out_ref[k] = r[...]


def combine_kernel(logits_ref, out_ref):
    logits = logits_ref[...]
    top = jnp.max(logits, axis=0, keepdims=True)
    powers = jnp.exp(logits - top)
    combine = (powers / jnp.sum(powers, axis=0, keepdims=True)).T
    high, low = pieces(combine, 2)
    out_ref[...] = jnp.concatenate([high, low, high], axis=1)


def expert_kernel(sent_ref, got_ref, in_high_ref, in_low_ref, out_high_ref, out_low_ref, out_ref):
    core = lax.axis_index("seq") % 2
    tiles, rows, _ = out_ref.shape
    half = tiles // 2
    experts = rows // SLOTS
    units = in_high_ref.shape[1] // experts
    near = join([sent_ref[0], got_ref[1]])
    far = join([sent_ref[1], got_ref[0]])
    near = [near[t] / near[half] for t in range(half)]
    far = [far[t] / far[half] for t in range(half)]
    first = [pick(core, a, b) for a, b in zip(near, far)]
    second = [pick(core, b, a) for a, b in zip(near, far)]
    inputs = stacked(jnp.concatenate(first + second, axis=1))
    large = mm(inputs, in_high_ref[...])
    small = mm(inputs, in_low_ref[...])
    value = large[:rows] + (large[rows:] + small[:rows])
    value = value * (1.0 + lax.erf(value * (0.5 ** 0.5))) * 0.5
    slot = lax.broadcasted_iota(jnp.int32, value.shape, 0)
    unit = lax.broadcasted_iota(jnp.int32, value.shape, 1)
    keep = None
    for e in range(experts):
        inside = (slot // SLOTS == e) & (unit >= e * units) & (unit < (e + 1) * units)
        keep = inside if keep is None else keep | inside
    hidden = stacked(jnp.where(keep, value, 0.0))
    large = mm(hidden, out_high_ref[...])
    small = mm(hidden, out_low_ref[...])
    out = large[:rows] + (large[rows:] + small[:rows])
    for t in range(tiles):
        out_ref[t] = out[:, t * LANES:(t + 1) * LANES]


def slot_pieces(parts, slots_ref):
    expert = lax.axis_index("expert")
    groups, (tiles, rows, _) = len(parts), parts[0].shape
    for k, part in enumerate(parts):
        place = pl.ds(pl.multiple_of(lax.rem(expert - k + groups, groups) * rows, rows), rows)
        for t in range(tiles):
            slots_ref[place, t * LANES:(t + 1) * LANES] = part[t]
    high, low = pieces(slots_ref[...], 2)
    return jnp.concatenate([high, high, low], axis=0)


def near_kernel(combine_ref, *refs):
    own_ref, others_ref, out_ref, slots_ref = refs
    parts = [own_ref[...]] + [others_ref[k] for k in range(others_ref.shape[0])]
    out_ref[...] = mm(combine_ref[...], slot_pieces(parts, slots_ref))


def far_kernel(combine_ref, own_ref, others_ref, near_ref, out_hbm, slots_ref, far_ref, sems):
    core = lax.axis_index("seq") % 2
    count, half = near_ref.shape
    columns = [pl.ds(pl.multiple_of(side * half, LANES), half) for side in (core, 1 - core)]
    copies = [pltpu.make_async_copy(near_ref, out_hbm.at[:, columns[0]], sems.at[0])]
    copies[0].start()
    parts = [own_ref[...]] + [others_ref[k] for k in range(others_ref.shape[0])]
    slots = slot_pieces(parts, slots_ref)
    step = pl.cdiv(count, 16 * (sems.shape[0] - 1)) * 16
    for i, start in enumerate(range(0, count, step)):
        size = min(step, count - start)
        far_ref[start:start + size] = mm(combine_ref[start:start + size], slots)
        place = pl.ds(start, size)
        copies.append(pltpu.make_async_copy(far_ref.at[place], out_hbm.at[place, columns[1]], sems.at[i + 1]))
        copies[-1].start()
    for copy in copies:
        copy.wait()


def solution(mesh):
    n_expert, n_seq, n_fsdp = (mesh.shape[a] for a in AXES)
    n_x = n_seq // 2

    def permute(value, target):
        pairs = []
        for e in range(n_expert):
            for s in range(n_seq):
                for f in range(n_fsdp):
                    te, tx, tc, tf = target(e, s // 2, s % 2, f)
                    pairs.append(((e * n_seq + s) * n_fsdp + f, (te * n_seq + tx * 2 + tc) * n_fsdp + tf))
        return lax.ppermute(value, AXES, pairs)

    def other_core(value):
        return permute(value, lambda e, x, c, f: (e, x, 1 - c, f))

    def along_ring(value, k):
        return permute(value, lambda e, x, c, f: (ring_step(e, k, n_expert), x, 1 - c, f))

    def around_expert(value, k):
        return permute(value, lambda e, x, c, f: ((e + k) % n_expert, x, 1 - c, f))

    def plane(value):
        return [
            permute(value, lambda e, x, c, f, dx=dx, df=df: (e, (x + dx) % n_x, 1 - c, (f + df) % n_fsdp))
            for dx in range(n_x)[::-1] for df in range(n_fsdp)[::-1] if dx or df
        ]

    def body(tokens, slot_params, w_in, w_out):
        count, width = tokens.shape
        slots = slot_params.shape[1]
        rows = w_in.shape[0] * SLOTS
        half = width // LANES // 2
        f32 = jnp.float32
        params = pltpu.CompilerParams(vmem_limit_bytes=24 * 1024 * 1024)
        core = lax.axis_index("seq") % 2
        step = count // 4 if count % 32 == 0 else count
        chunks = [(i, i + step) for i in range(0, count, step)]
        in_hbm = lambda value: pltpu.with_memory_space_constraint(value, pltpu.HBM)
        shape = pltpu.VMEM((n_expert, half + 2, rows, LANES), f32)
        logits, mine, theirs, w_in = pl.pallas_call(
            functools.partial(dispatch_kernel, chunks),
            out_shape=(pltpu.VMEM((slots, count), f32), shape, shape, pltpu.VMEM(w_in.shape, f32)),
            in_specs=[HBM, HBM, HBM],
            out_specs=(VMEM,) * 4,
            scratch_shapes=[
                pltpu.VMEM((count, width), f32),
                pltpu.VMEM((slots, width), f32),
                pltpu.VMEM((slots, width + 2 * LANES), f32),
                pltpu.SemaphoreType.DMA((len(chunks) + 2,)),
            ],
            compiler_params=params,
        )(in_hbm(tokens), in_hbm(slot_params.T), in_hbm(w_in))
        combine = pl.pallas_call(
            combine_kernel,
            out_shape=jax.ShapeDtypeStruct((count, 3 * slots), jnp.bfloat16),
            in_specs=[VMEM],
            out_specs=VMEM,
            compiler_params=params,
        )(logits)

        chip = pl.pallas_call(
            chip_kernel,
            out_shape=(pltpu.VMEM((half + 2, rows, LANES), f32),) * n_expert,
            in_specs=[VMEM, VMEM],
            out_specs=(VMEM,) * n_expert,
            compiler_params=params,
        )(mine, other_core(theirs))
        flag = pltpu.VMEM((8, LANES), f32)
        experts, units, _ = w_in.shape
        cost = pl.CostEstimate(flops=8 * w_in.size, bytes_accessed=8 * w_in.size, transcendentals=0)

        def local(kernel, out, *args):
            return pl.pallas_call(
                kernel,
                out_shape=out,
                in_specs=[VMEM] * len(args),
                out_specs=jax.tree.map(lambda _: VMEM, out),
                compiler_params=params,
            )(*args)

        part = pltpu.VMEM((experts * units, width), jnp.bfloat16)
        parts = 4 if units % 64 == 0 else 1
        out_high, out_low, ready = pl.pallas_call(
            split_out_kernel,
            out_shape=(part, part, flag),
            in_specs=[VMEM, HBM],
            out_specs=(VMEM,) * 3,
            scratch_shapes=[pltpu.VMEM(w_out.shape, f32), pltpu.SemaphoreType.DMA((experts * parts,))],
            cost_estimate=cost,
            compiler_params=params,
        )(chip[0], in_hbm(w_out))
        shape = pltpu.VMEM((half + 2, rows, LANES), f32)
        total = local(total_kernel, shape, chip[0], *[along_ring(chip[k], k) for k in range(1, n_expert)], ready)
        part = pltpu.VMEM((width, experts * units), jnp.bfloat16)
        in_high, in_low, ready = pl.pallas_call(
            split_in_kernel,
            out_shape=(part, part, flag),
            in_specs=[VMEM, VMEM],
            out_specs=(VMEM,) * 3,
            cost_estimate=cost,
            compiler_params=params,
        )(total, w_in)
        shape = pltpu.VMEM((2, half + 2, rows, LANES), f32)
        sent = local(plane_kernel, shape, total, *plane(total), ready)
        shape = pltpu.VMEM((2 * half, rows, LANES), f32)
        partial = local(expert_kernel, shape, sent, other_core(sent), in_high, in_low, out_high, out_low)
        shape = pltpu.VMEM((half, rows, LANES), f32)
        keep, send = local(halves_kernel, (shape, shape), partial, other_core(partial))
        around = plane(send)
        own = local(add_kernel, shape, keep, *around[-1:], *around[:-1])
        arrived = [around_expert(own, k) for k in range(1, n_expert)]
        own_near = other_core(own)
        shape = pltpu.VMEM((n_expert - 1, half, rows, LANES), f32)
        others = local(stack_kernel, shape, combine, *arrived, own_near)
        whole = pltpu.VMEM((count, half * LANES), f32)
        slot_values = pltpu.VMEM((slots, half * LANES), f32)
        near = pl.pallas_call(
            near_kernel,
            out_shape=whole,
            in_specs=[VMEM] * 3,
            out_specs=VMEM,
            scratch_shapes=[slot_values],
            compiler_params=params,
        )(combine, own_near, others)
        return pl.pallas_call(
            far_kernel,
            out_shape=jax.ShapeDtypeStruct((count, width), f32),
            in_specs=[VMEM] * 4,
            out_specs=HBM,
            scratch_shapes=[slot_values, whole, pltpu.SemaphoreType.DMA((5,))],
            compiler_params=params,
        )(combine, own, other_core(others), near)

    return jax.shard_map(
        body,
        mesh=mesh,
        in_specs=(P(AXES, None), P(), P("expert", ("seq", "fsdp"), None), P("expert", ("seq", "fsdp"), None)),
        out_specs=P(AXES, None),
        check_vma=False,
    )
```

```python
import functools

import jax
import jax.numpy as jnp
from jax import lax
from jax.experimental import pallas as pl
from jax.experimental.pallas import tpu as pltpu
from jax.sharding import PartitionSpec as P

SLOTS = 4
LANES = 128
AXES = ("expert", "seq", "fsdp")
VMEM = pl.BlockSpec(memory_space=pltpu.VMEM)
HBM = pl.BlockSpec(memory_space=pltpu.HBM)


def pieces(value, count):
    out = []
    for _ in range(count):
        part = value.astype(jnp.bfloat16)
        out.append(part)
        value = value - part.astype(jnp.float32)
    return out


def stacked(value):
    high, low = pieces(value, 2)
    return jnp.concatenate([high.astype(jnp.float32), low.astype(jnp.float32)], axis=0).astype(jnp.bfloat16)


def mm(left, right, contract=((1,), (0,))):
    return lax.dot_general(left, right, (contract, ((), ())), preferred_element_type=jnp.float32)


def pick(core, when_zero, when_one):
    return jnp.where(core == 0, when_zero, when_one)


def join(parts):
    top = functools.reduce(jnp.maximum, [p[-1] for p in parts])
    total = sum(p[:-1] * jnp.exp(p[-1] - top)[None] for p in parts)
    return jnp.concatenate([total, top[None]], axis=0)


def dispatch_kernel(chunks, tokens_hbm, params_hbm, w_in_hbm, logits_ref, mine_ref, theirs_ref, w_in_ref,
                    tokens_ref, params_ref, sums_ref, sems):
    core, expert = lax.axis_index("seq") % 2, lax.axis_index("expert")
    groups, tiles, rows, _ = mine_ref.shape
    half = tiles - 2
    slots, width = params_hbm.shape
    copies = [pltpu.make_async_copy(params_hbm, params_ref, sems.at[0])]
    for start, stop in chunks:
        own = pl.ds(start, stop - start)
        copies.append(pltpu.make_async_copy(tokens_hbm.at[own], tokens_ref.at[own], sems.at[len(copies)]))
    copies.append(pltpu.make_async_copy(w_in_hbm, w_in_ref, sems.at[len(copies)]))
    for copy in copies:
        copy.start()
    copies[0].wait()
    params = jnp.concatenate(pieces(params_ref[...], 3), axis=0)
    for copy in copies[1:-1]:
        copy.wait()
    token_high, token_low, rest = pieces(tokens_ref[...], 3)
    nt = ((1,), (1,))
    a = mm(params, token_high, nt)
    b = mm(params[:2 * slots], token_low, nt)
    c = mm(params[:slots], rest, nt)
    small = a[2 * slots:] + b[slots:] + c
    logits = (small + (a[slots:2 * slots] + b[:slots])) + a[:slots]
    logits_ref[...] = logits
    peak = jnp.max(logits, axis=1, keepdims=True)
    weights = jnp.exp(logits - peak)
    mass = jnp.sum(weights, axis=1, keepdims=True)
    weight_high, weight_low = pieces(weights, 2)
    high = mm(jnp.concatenate([weight_high, weight_low], axis=0), token_high)
    low = mm(weight_high, token_low)
    sums_ref[:, :width] = high[:slots] + (high[slots:] + low)
    sums_ref[:, width:width + LANES] = jnp.broadcast_to(mass, (slots, LANES))
    sums_ref[:, width + LANES:] = jnp.broadcast_to(peak, (slots, LANES))
    for k in range(groups):
        own = pl.ds(pl.multiple_of((expert ^ k) * rows, rows), rows)
        sides = (core, 1 - core) if k else (1 - core, core)
        for ref, side in zip((mine_ref, theirs_ref), sides):
            for t in range(half):
                place = pl.ds(pl.multiple_of((side * half + t) * LANES, LANES), LANES)
                ref[k, t] = sums_ref[own, place]
            for t in range(2):
                ref[k, half + t] = sums_ref[own, width + t * LANES:width + (t + 1) * LANES]
    copies[-1].wait()


def chip_kernel(mine_ref, theirs_ref, *outs):
    for k, out_ref in enumerate(outs):
        out_ref[...] = join([mine_ref[k], theirs_ref[k]])


def split_out_kernel(_, w_hbm, high_ref, low_ref, flag_ref, w_ref, sems):
    experts, units, _ = w_hbm.shape
    parts = sems.shape[0] // experts
    count = units // parts
    copies = []
    for e in range(experts):
        for i in range(parts):
            own = pl.ds(i * count, count)
            copies.append(pltpu.make_async_copy(w_hbm.at[e, own], w_ref.at[e, own], sems.at[len(copies)]))
            copies[-1].start()
    for e in range(experts):
        for i in range(parts):
            copies[e * parts + i].wait()
            start = e * units + i * count
            own = slice(start, start + count)
            high_ref[own], low_ref[own] = pieces(w_ref[e, i * count:(i + 1) * count], 2)
    flag_ref[...] = jnp.zeros_like(flag_ref)


def split_in_kernel(_, w_ref, high_ref, low_ref, flag_ref):
    experts, units, width = w_ref.shape
    high, low = pieces(w_ref[...].reshape(experts * units, width), 2)
    high_ref[...] = high.T
    low_ref[...] = low.T
    flag_ref[...] = jnp.zeros_like(flag_ref)


def total_kernel(own_ref, *refs):
    *others, _, out_ref = refs
    out_ref[...] = join([own_ref[...]] + [r[...] for r in others])


def plane_kernel(own_ref, *refs):
    *others, _, out_ref = refs
    out_ref[0] = join([r[...] for r in others])
    out_ref[1] = own_ref[...]


def halves_kernel(mine_ref, theirs_ref, keep_ref, send_ref):
    core = lax.axis_index("seq") % 2
    half = keep_ref.shape[0]
    for ref, side in ((send_ref, core), (keep_ref, 1 - core)):
        own = pl.ds(side * half, half)
        ref[...] = mine_ref[own] + theirs_ref[own]


def add_kernel(own_ref, *refs):
    *others, out_ref = refs
    out_ref[...] = own_ref[...] + sum(r[...] for r in others)


def stack_kernel(*refs):
    _, *others, _, out_ref = refs
    for k, r in enumerate(others):
        out_ref[k] = r[...]


def combine_kernel(logits_ref, out_ref):
    logits = logits_ref[...]
    top = jnp.max(logits, axis=0, keepdims=True)
    powers = jnp.exp(logits - top)
    combine = (powers / jnp.sum(powers, axis=0, keepdims=True)).T
    high, low = pieces(combine, 2)
    out_ref[...] = jnp.concatenate([high, low, high], axis=1)


def expert_kernel(sent_ref, got_ref, in_high_ref, in_low_ref, out_high_ref, out_low_ref, out_ref):
    core = lax.axis_index("seq") % 2
    tiles, rows, _ = out_ref.shape
    half = tiles // 2
    experts = rows // SLOTS
    units = in_high_ref.shape[1] // experts
    near = join([sent_ref[0], got_ref[1]])
    far = join([sent_ref[1], got_ref[0]])
    near = [near[t] / near[half] for t in range(half)]
    far = [far[t] / far[half] for t in range(half)]
    first = [pick(core, a, b) for a, b in zip(near, far)]
    second = [pick(core, b, a) for a, b in zip(near, far)]
    inputs = stacked(jnp.concatenate(first + second, axis=1))
    large = mm(inputs, in_high_ref[...])
    small = mm(inputs, in_low_ref[...])
    value = large[:rows] + (large[rows:] + small[:rows])
    value = value * (1.0 + lax.erf(value * (0.5 ** 0.5))) * 0.5
    slot = lax.broadcasted_iota(jnp.int32, value.shape, 0)
    unit = lax.broadcasted_iota(jnp.int32, value.shape, 1)
    keep = None
    for e in range(experts):
        inside = (slot // SLOTS == e) & (unit >= e * units) & (unit < (e + 1) * units)
        keep = inside if keep is None else keep | inside
    hidden = stacked(jnp.where(keep, value, 0.0))
    large = mm(hidden, out_high_ref[...])
    small = mm(hidden, out_low_ref[...])
    out = large[:rows] + (large[rows:] + small[:rows])
    for t in range(tiles):
        out_ref[t] = out[:, t * LANES:(t + 1) * LANES]


def mix_kernel(near, combine_ref, own_ref, others_ref, *refs):
    out_hbm, slots_ref, out_ref, sems = refs[-4:]
    core, expert = lax.axis_index("seq") % 2, lax.axis_index("expert")
    half, rows, _ = own_ref.shape
    groups = others_ref.shape[0] + 1
    for k in range(groups):
        place = pl.ds(pl.multiple_of(lax.rem(expert - k + groups, groups) * rows, rows), rows)
        for t in range(half):
            slots_ref[place, t * LANES:(t + 1) * LANES] = others_ref[k - 1, t] if k else own_ref[t]
    high, low = pieces(slots_ref[...], 2)
    slots = jnp.concatenate([high, high, low], axis=0)
    side = core if near else 1 - core
    columns = pl.ds(pl.multiple_of(side * (half * LANES), LANES), half * LANES)
    count = combine_ref.shape[0]
    step = pl.cdiv(count, 16 * sems.shape[0]) * 16
    copies = []
    for i, start in enumerate(range(0, count, step)):
        size = min(step, count - start)
        out_ref[start:start + size] = mm(combine_ref[start:start + size], slots)
        place = pl.ds(start, size)
        copies.append(pltpu.make_async_copy(out_ref.at[place], out_hbm.at[place, columns], sems.at[i]))
        copies[i].start()
    for copy in copies:
        copy.wait()


def solution(mesh):
    n_expert, n_seq, n_fsdp = (mesh.shape[a] for a in AXES)
    n_x = n_seq // 2

    def permute(value, target):
        pairs = []
        for e in range(n_expert):
            for s in range(n_seq):
                for f in range(n_fsdp):
                    te, tx, tc, tf = target(e, s // 2, s % 2, f)
                    pairs.append(((e * n_seq + s) * n_fsdp + f, (te * n_seq + tx * 2 + tc) * n_fsdp + tf))
        return lax.ppermute(value, AXES, pairs)

    def other_core(value):
        return permute(value, lambda e, x, c, f: (e, x, 1 - c, f))

    def along_expert(value, k):
        return permute(value, lambda e, x, c, f: (e ^ k, x, 1 - c, f))

    def around_expert(value, k):
        return permute(value, lambda e, x, c, f: ((e + k) % n_expert, x, 1 - c, f))

    def plane(value):
        return [
            permute(value, lambda e, x, c, f, dx=dx, df=df: (e, (x + dx) % n_x, 1 - c, (f + df) % n_fsdp))
            for dx in range(n_x)[::-1] for df in range(n_fsdp)[::-1] if dx or df
        ]

    def body(tokens, slot_params, w_in, w_out):
        count, width = tokens.shape
        slots = slot_params.shape[1]
        rows = w_in.shape[0] * SLOTS
        half = width // LANES // 2
        f32 = jnp.float32
        params = pltpu.CompilerParams(vmem_limit_bytes=24 * 1024 * 1024)
        core = lax.axis_index("seq") % 2
        step = count // 4 if count % 32 == 0 else count
        chunks = [(i, i + step) for i in range(0, count, step)]
        in_hbm = lambda value: pltpu.with_memory_space_constraint(value, pltpu.HBM)
        shape = pltpu.VMEM((n_expert, half + 2, rows, LANES), f32)
        logits, mine, theirs, w_in = pl.pallas_call(
            functools.partial(dispatch_kernel, chunks),
            out_shape=(pltpu.VMEM((slots, count), f32), shape, shape, pltpu.VMEM(w_in.shape, f32)),
            in_specs=[HBM, HBM, HBM],
            out_specs=(VMEM,) * 4,
            scratch_shapes=[
                pltpu.VMEM((count, width), f32),
                pltpu.VMEM((slots, width), f32),
                pltpu.VMEM((slots, width + 2 * LANES), f32),
                pltpu.SemaphoreType.DMA((len(chunks) + 2,)),
            ],
            compiler_params=params,
        )(in_hbm(tokens), in_hbm(slot_params.T), in_hbm(w_in))
        combine = pl.pallas_call(
            combine_kernel,
            out_shape=jax.ShapeDtypeStruct((count, 3 * slots), jnp.bfloat16),
            in_specs=[VMEM],
            out_specs=VMEM,
            compiler_params=params,
        )(logits)

        chip = pl.pallas_call(
            chip_kernel,
            out_shape=(pltpu.VMEM((half + 2, rows, LANES), f32),) * n_expert,
            in_specs=[VMEM, VMEM],
            out_specs=(VMEM,) * n_expert,
            compiler_params=params,
        )(mine, other_core(theirs))
        order = sorted(range(n_expert - 1, 0, -1), key=lambda k: k != n_expert // 2)
        flag = pltpu.VMEM((8, LANES), f32)
        experts, units, _ = w_in.shape
        cost = pl.CostEstimate(flops=8 * w_in.size, bytes_accessed=8 * w_in.size, transcendentals=0)

        def local(kernel, out, *args):
            return pl.pallas_call(
                kernel,
                out_shape=out,
                in_specs=[VMEM] * len(args),
                out_specs=jax.tree.map(lambda _: VMEM, out),
                compiler_params=params,
            )(*args)

        part = pltpu.VMEM((experts * units, width), jnp.bfloat16)
        parts = 4 if units % 64 == 0 else 1
        out_high, out_low, ready = pl.pallas_call(
            split_out_kernel,
            out_shape=(part, part, flag),
            in_specs=[VMEM, HBM],
            out_specs=(VMEM,) * 3,
            scratch_shapes=[pltpu.VMEM(w_out.shape, f32), pltpu.SemaphoreType.DMA((experts * parts,))],
            cost_estimate=cost,
            compiler_params=params,
        )(chip[0], in_hbm(w_out))
        shape = pltpu.VMEM((half + 2, rows, LANES), f32)
        total = local(total_kernel, shape, chip[0], *[along_expert(chip[k], k) for k in order], ready)
        part = pltpu.VMEM((width, experts * units), jnp.bfloat16)
        in_high, in_low, ready = pl.pallas_call(
            split_in_kernel,
            out_shape=(part, part, flag),
            in_specs=[VMEM, VMEM],
            out_specs=(VMEM,) * 3,
            cost_estimate=cost,
            compiler_params=params,
        )(total, w_in)
        shape = pltpu.VMEM((2, half + 2, rows, LANES), f32)
        sent = local(plane_kernel, shape, total, *plane(total), ready)
        shape = pltpu.VMEM((2 * half, rows, LANES), f32)
        partial = local(expert_kernel, shape, sent, other_core(sent), in_high, in_low, out_high, out_low)
        shape = pltpu.VMEM((half, rows, LANES), f32)
        keep, send = local(halves_kernel, (shape, shape), partial, other_core(partial))
        around = plane(send)
        own = local(add_kernel, shape, keep, *around[-1:], *around[:-1])
        arrived = [around_expert(own, k) for k in range(1, n_expert)]
        own_near = other_core(own)
        shape = pltpu.VMEM((n_expert - 1, half, rows, LANES), f32)
        others = local(stack_kernel, shape, combine, *arrived, own_near)

        def mix(near, own, others, *out):
            return pl.pallas_call(
                functools.partial(mix_kernel, near),
                out_shape=jax.ShapeDtypeStruct((count, width), f32),
                in_specs=[VMEM, VMEM, VMEM] + [HBM] * len(out),
                out_specs=HBM,
                scratch_shapes=[
                    pltpu.VMEM((slots, half * LANES), f32),
                    pltpu.VMEM((count, half * LANES), f32),
                    pltpu.SemaphoreType.DMA((4,)),
                ],
                input_output_aliases={3: 0} if out else {},
                compiler_params=params,
            )(combine, own, others, *out)

        mixed = mix(True, own_near, others)
        return mix(False, own, other_core(others), mixed)

    return jax.shard_map(
        body,
        mesh=mesh,
        in_specs=(P(AXES, None), P(), P("expert", ("seq", "fsdp"), None), P("expert", ("seq", "fsdp"), None)),
        out_specs=P(AXES, None),
        check_vma=False,
    )
```

```python
import functools

import jax
import jax.numpy as jnp
from jax import lax
from jax.experimental import pallas as pl
from jax.experimental.pallas import tpu as pltpu
from jax.sharding import PartitionSpec as P

SLOTS = 4
LANES = 128
AXES = ("expert", "seq", "fsdp")
VMEM = pl.BlockSpec(memory_space=pltpu.VMEM)
HBM = pl.BlockSpec(memory_space=pltpu.HBM)


def pieces(value, count):
    out = []
    for _ in range(count):
        part = value.astype(jnp.bfloat16)
        out.append(part)
        value = value - part.astype(jnp.float32)
    return out


def stacked(value):
    high, low = pieces(value, 2)
    return jnp.concatenate([high.astype(jnp.float32), low.astype(jnp.float32)], axis=0).astype(jnp.bfloat16)


def mm(left, right, contract=((1,), (0,))):
    return lax.dot_general(left, right, (contract, ((), ())), preferred_element_type=jnp.float32)


def pick(core, when_zero, when_one):
    return jnp.where(core == 0, when_zero, when_one)


def join(parts):
    top = functools.reduce(jnp.maximum, [p[-1] for p in parts])
    total = sum(p[:-1] * jnp.exp(p[-1] - top)[None] for p in parts)
    return jnp.concatenate([total, top[None]], axis=0)


def dispatch_kernel(chunks, tokens_hbm, params_hbm, w_in_hbm, logits_ref, mine_ref, theirs_ref, w_in_ref,
                    tokens_ref, params_ref, sums_ref, sems):
    core, expert = lax.axis_index("seq") % 2, lax.axis_index("expert")
    groups, tiles, rows, _ = mine_ref.shape
    half = tiles - 2
    slots, width = params_hbm.shape
    copies = [pltpu.make_async_copy(params_hbm, params_ref, sems.at[0])]
    for start, stop in chunks:
        own = pl.ds(start, stop - start)
        copies.append(pltpu.make_async_copy(tokens_hbm.at[own], tokens_ref.at[own], sems.at[len(copies)]))
    copies.append(pltpu.make_async_copy(w_in_hbm, w_in_ref, sems.at[len(copies)]))
    for copy in copies:
        copy.start()
    copies[0].wait()
    params = jnp.concatenate(pieces(params_ref[...], 3), axis=0)
    for copy in copies[1:-1]:
        copy.wait()
    token_high, token_low, rest = pieces(tokens_ref[...], 3)
    nt = ((1,), (1,))
    a = mm(params, token_high, nt)
    b = mm(params[:2 * slots], token_low, nt)
    c = mm(params[:slots], rest, nt)
    small = a[2 * slots:] + b[slots:] + c
    logits = (small + (a[slots:2 * slots] + b[:slots])) + a[:slots]
    logits_ref[...] = logits
    peak = jnp.max(logits, axis=1, keepdims=True)
    weights = jnp.exp(logits - peak)
    mass = jnp.sum(weights, axis=1, keepdims=True)
    weight_high, weight_low = pieces(weights, 2)
    high = mm(jnp.concatenate([weight_high, weight_low], axis=0), token_high)
    low = mm(weight_high, token_low)
    sums_ref[:, :width] = high[:slots] + (high[slots:] + low)
    sums_ref[:, width:width + LANES] = jnp.broadcast_to(mass, (slots, LANES))
    sums_ref[:, width + LANES:] = jnp.broadcast_to(peak, (slots, LANES))
    for k in range(groups):
        own = pl.ds(pl.multiple_of((expert ^ k) * rows, rows), rows)
        sides = (core, 1 - core) if k else (1 - core, core)
        for ref, side in zip((mine_ref, theirs_ref), sides):
            for t in range(half):
                place = pl.ds(pl.multiple_of((side * half + t) * LANES, LANES), LANES)
                ref[k, t] = sums_ref[own, place]
            for t in range(2):
                ref[k, half + t] = sums_ref[own, width + t * LANES:width + (t + 1) * LANES]
    copies[-1].wait()


def chip_kernel(mine_ref, theirs_ref, *outs):
    for k, out_ref in enumerate(outs):
        out_ref[...] = join([mine_ref[k], theirs_ref[k]])


def split_out_kernel(_, w_hbm, high_ref, low_ref, flag_ref, w_ref, sems):
    experts, units, _ = w_hbm.shape
    parts = sems.shape[0] // experts
    count = units // parts
    copies = []
    for e in range(experts):
        for i in range(parts):
            own = pl.ds(i * count, count)
            copies.append(pltpu.make_async_copy(w_hbm.at[e, own], w_ref.at[e, own], sems.at[len(copies)]))
            copies[-1].start()
    for e in range(experts):
        for i in range(parts):
            copies[e * parts + i].wait()
            start = e * units + i * count
            own = slice(start, start + count)
            high_ref[own], low_ref[own] = pieces(w_ref[e, i * count:(i + 1) * count], 2)
    flag_ref[...] = jnp.zeros_like(flag_ref)


def split_in_kernel(_, w_ref, high_ref, low_ref, flag_ref):
    experts, units, width = w_ref.shape
    high, low = pieces(w_ref[...].reshape(experts * units, width), 2)
    high_ref[...] = high.T
    low_ref[...] = low.T
    flag_ref[...] = jnp.zeros_like(flag_ref)


def total_kernel(own_ref, *refs):
    *others, _, out_ref = refs
    out_ref[...] = join([own_ref[...]] + [r[...] for r in others])


def plane_kernel(own_ref, *refs):
    *others, _, out_ref = refs
    out_ref[0] = join([r[...] for r in others])
    out_ref[1] = own_ref[...]


def halves_kernel(mine_ref, theirs_ref, keep_ref, send_ref):
    core = lax.axis_index("seq") % 2
    half = keep_ref.shape[0]
    for ref, side in ((send_ref, core), (keep_ref, 1 - core)):
        own = pl.ds(side * half, half)
        ref[...] = mine_ref[own] + theirs_ref[own]


def add_kernel(own_ref, *refs):
    *others, out_ref = refs
    out_ref[...] = own_ref[...] + sum(r[...] for r in others)


def stack_kernel(*refs):
    _, *others, _, out_ref = refs
    for k, r in enumerate(others):
        out_ref[k] = r[...]


def combine_kernel(logits_ref, out_ref):
    logits = logits_ref[...]
    top = jnp.max(logits, axis=0, keepdims=True)
    powers = jnp.exp(logits - top)
    combine = (powers / jnp.sum(powers, axis=0, keepdims=True)).T
    high, low = pieces(combine, 2)
    out_ref[...] = jnp.concatenate([high, low, high], axis=1)


def expert_kernel(sent_ref, got_ref, in_high_ref, in_low_ref, out_high_ref, out_low_ref, out_ref):
    core = lax.axis_index("seq") % 2
    tiles, rows, _ = out_ref.shape
    half = tiles // 2
    experts = rows // SLOTS
    units = in_high_ref.shape[1] // experts
    near = join([sent_ref[0], got_ref[1]])
    far = join([sent_ref[1], got_ref[0]])
    near = [near[t] / near[half] for t in range(half)]
    far = [far[t] / far[half] for t in range(half)]
    first = [pick(core, a, b) for a, b in zip(near, far)]
    second = [pick(core, b, a) for a, b in zip(near, far)]
    inputs = stacked(jnp.concatenate(first + second, axis=1))
    large = mm(inputs, in_high_ref[...])
    small = mm(inputs, in_low_ref[...])
    value = large[:rows] + (large[rows:] + small[:rows])
    value = value * (1.0 + lax.erf(value * (0.5 ** 0.5))) * 0.5
    slot = lax.broadcasted_iota(jnp.int32, value.shape, 0)
    unit = lax.broadcasted_iota(jnp.int32, value.shape, 1)
    keep = None
    for e in range(experts):
        inside = (slot // SLOTS == e) & (unit >= e * units) & (unit < (e + 1) * units)
        keep = inside if keep is None else keep | inside
    hidden = stacked(jnp.where(keep, value, 0.0))
    large = mm(hidden, out_high_ref[...])
    small = mm(hidden, out_low_ref[...])
    out = large[:rows] + (large[rows:] + small[:rows])
    for t in range(tiles):
        out_ref[t] = out[:, t * LANES:(t + 1) * LANES]


def mix_kernel(near, combine_ref, own_ref, others_ref, *refs):
    out_hbm, slots_ref, out_ref, sems = refs[-4:]
    core, expert = lax.axis_index("seq") % 2, lax.axis_index("expert")
    half, rows, _ = own_ref.shape
    groups = others_ref.shape[0] + 1
    for k in range(groups):
        place = pl.ds(pl.multiple_of(lax.rem(expert - k + groups, groups) * rows, rows), rows)
        for t in range(half):
            slots_ref[place, t * LANES:(t + 1) * LANES] = others_ref[k - 1, t] if k else own_ref[t]
    high, low = pieces(slots_ref[...], 2)
    slots = jnp.concatenate([high, high, low], axis=0)
    side = core if near else 1 - core
    columns = pl.ds(pl.multiple_of(side * (half * LANES), LANES), half * LANES)
    count = combine_ref.shape[0]
    step = pl.cdiv(count, 16 * sems.shape[0]) * 16
    copies = []
    for i, start in enumerate(range(0, count, step)):
        size = min(step, count - start)
        out_ref[start:start + size] = mm(combine_ref[start:start + size], slots)
        place = pl.ds(start, size)
        copies.append(pltpu.make_async_copy(out_ref.at[place], out_hbm.at[place, columns], sems.at[i]))
        copies[i].start()
    for copy in copies:
        copy.wait()


def solution(mesh):
    n_expert, n_seq, n_fsdp = (mesh.shape[a] for a in AXES)
    n_x = n_seq // 2

    def permute(value, target):
        pairs = []
        for e in range(n_expert):
            for s in range(n_seq):
                for f in range(n_fsdp):
                    te, tx, tc, tf = target(e, s // 2, s % 2, f)
                    pairs.append(((e * n_seq + s) * n_fsdp + f, (te * n_seq + tx * 2 + tc) * n_fsdp + tf))
        return lax.ppermute(value, AXES, pairs)

    def other_core(value):
        return permute(value, lambda e, x, c, f: (e, x, 1 - c, f))

    def along_expert(value, k):
        return permute(value, lambda e, x, c, f: (e ^ k, x, 1 - c, f))

    def around_expert(value, k):
        return permute(value, lambda e, x, c, f: ((e + k) % n_expert, x, 1 - c, f))

    def plane(value):
        return [
            permute(value, lambda e, x, c, f, dx=dx, df=df: (e, (x + dx) % n_x, 1 - c, (f + df) % n_fsdp))
            for dx in range(n_x)[::-1] for df in range(n_fsdp)[::-1] if dx or df
        ]

    def turned(value):
        return [
            permute(value, lambda e, x, c, f: (e, 1 - x, 1 - c, 1 - f)),
            permute(value, lambda e, x, c, f: (e, f, 1 - c, 1 - x)),
            permute(value, lambda e, x, c, f: (e, 1 - f, 1 - c, x)),
        ]

    def body(tokens, slot_params, w_in, w_out):
        count, width = tokens.shape
        slots = slot_params.shape[1]
        rows = w_in.shape[0] * SLOTS
        half = width // LANES // 2
        f32 = jnp.float32
        params = pltpu.CompilerParams(vmem_limit_bytes=24 * 1024 * 1024)
        core = lax.axis_index("seq") % 2
        step = count // 4 if count % 32 == 0 else count
        chunks = [(i, i + step) for i in range(0, count, step)]
        in_hbm = lambda value: pltpu.with_memory_space_constraint(value, pltpu.HBM)
        shape = pltpu.VMEM((n_expert, half + 2, rows, LANES), f32)
        logits, mine, theirs, w_in = pl.pallas_call(
            functools.partial(dispatch_kernel, chunks),
            out_shape=(pltpu.VMEM((slots, count), f32), shape, shape, pltpu.VMEM(w_in.shape, f32)),
            in_specs=[HBM, HBM, HBM],
            out_specs=(VMEM,) * 4,
            scratch_shapes=[
                pltpu.VMEM((count, width), f32),
                pltpu.VMEM((slots, width), f32),
                pltpu.VMEM((slots, width + 2 * LANES), f32),
                pltpu.SemaphoreType.DMA((len(chunks) + 2,)),
            ],
            compiler_params=params,
        )(in_hbm(tokens), in_hbm(slot_params.T), in_hbm(w_in))
        combine = pl.pallas_call(
            combine_kernel,
            out_shape=jax.ShapeDtypeStruct((count, 3 * slots), jnp.bfloat16),
            in_specs=[VMEM],
            out_specs=VMEM,
            compiler_params=params,
        )(logits)

        chip = pl.pallas_call(
            chip_kernel,
            out_shape=(pltpu.VMEM((half + 2, rows, LANES), f32),) * n_expert,
            in_specs=[VMEM, VMEM],
            out_specs=(VMEM,) * n_expert,
            compiler_params=params,
        )(mine, other_core(theirs))
        order = list(range(n_expert - 1, 0, -1))
        flag = pltpu.VMEM((8, LANES), f32)
        experts, units, _ = w_in.shape
        cost = pl.CostEstimate(flops=8 * w_in.size, bytes_accessed=8 * w_in.size, transcendentals=0)

        def local(kernel, out, *args):
            return pl.pallas_call(
                kernel,
                out_shape=out,
                in_specs=[VMEM] * len(args),
                out_specs=jax.tree.map(lambda _: VMEM, out),
                compiler_params=params,
            )(*args)

        part = pltpu.VMEM((experts * units, width), jnp.bfloat16)
        parts = 4 if units % 64 == 0 else 1
        out_high, out_low, ready = pl.pallas_call(
            split_out_kernel,
            out_shape=(part, part, flag),
            in_specs=[VMEM, HBM],
            out_specs=(VMEM,) * 3,
            scratch_shapes=[pltpu.VMEM(w_out.shape, f32), pltpu.SemaphoreType.DMA((experts * parts,))],
            cost_estimate=cost,
            compiler_params=params,
        )(chip[0], in_hbm(w_out))
        shape = pltpu.VMEM((half + 2, rows, LANES), f32)
        total = local(total_kernel, shape, chip[0], *[along_expert(chip[k], k) for k in order], ready)
        part = pltpu.VMEM((width, experts * units), jnp.bfloat16)
        in_high, in_low, ready = pl.pallas_call(
            split_in_kernel,
            out_shape=(part, part, flag),
            in_specs=[VMEM, VMEM],
            out_specs=(VMEM,) * 3,
            cost_estimate=cost,
            compiler_params=params,
        )(total, w_in)
        shape = pltpu.VMEM((2, half + 2, rows, LANES), f32)
        sent = local(plane_kernel, shape, total, *plane(total), ready)
        shape = pltpu.VMEM((2 * half, rows, LANES), f32)
        partial = local(expert_kernel, shape, sent, other_core(sent), in_high, in_low, out_high, out_low)
        shape = pltpu.VMEM((half, rows, LANES), f32)
        keep, send = local(halves_kernel, (shape, shape), partial, other_core(partial))
        around = turned(send) if n_x == n_fsdp == 2 else plane(send)
        own = local(add_kernel, shape, keep, *around[-1:], *around[:-1])
        arrived = [around_expert(own, k) for k in range(1, n_expert)]
        own_near = other_core(own)
        shape = pltpu.VMEM((n_expert - 1, half, rows, LANES), f32)
        others = local(stack_kernel, shape, combine, *arrived, own_near)

        def mix(near, own, others, *out):
            return pl.pallas_call(
                functools.partial(mix_kernel, near),
                out_shape=jax.ShapeDtypeStruct((count, width), f32),
                in_specs=[VMEM, VMEM, VMEM] + [HBM] * len(out),
                out_specs=HBM,
                scratch_shapes=[
                    pltpu.VMEM((slots, half * LANES), f32),
                    pltpu.VMEM((count, half * LANES), f32),
                    pltpu.SemaphoreType.DMA((4,)),
                ],
                input_output_aliases={3: 0} if out else {},
                compiler_params=params,
            )(combine, own, others, *out)

        mixed = mix(True, own_near, others)
        return mix(False, own, other_core(others), mixed)

    return jax.shard_map(
        body,
        mesh=mesh,
        in_specs=(P(AXES, None), P(), P("expert", ("seq", "fsdp"), None), P("expert", ("seq", "fsdp"), None)),
        out_specs=P(AXES, None),
        check_vma=False,
    )
```

```python
import functools

import jax
import jax.numpy as jnp
from jax import lax
from jax.experimental import pallas as pl
from jax.experimental.pallas import tpu as pltpu
from jax.sharding import PartitionSpec as P

SLOTS = 4
LANES = 128
AXES = ("expert", "seq", "fsdp")
VMEM = pl.BlockSpec(memory_space=pltpu.VMEM)
HBM = pl.BlockSpec(memory_space=pltpu.HBM)


def pieces(value, count):
    out = []
    for _ in range(count):
        part = value.astype(jnp.bfloat16)
        out.append(part)
        value = value - part.astype(jnp.float32)
    return out


def stacked(value):
    high, low = pieces(value, 2)
    return jnp.concatenate([high.astype(jnp.float32), low.astype(jnp.float32)], axis=0).astype(jnp.bfloat16)


def mm(left, right, contract=((1,), (0,))):
    return lax.dot_general(left, right, (contract, ((), ())), preferred_element_type=jnp.float32)


def pick(core, when_zero, when_one):
    return jnp.where(core == 0, when_zero, when_one)


def ring_step(e, k, n, where=lambda c, a, b: a if c else b):
    place = where(e % 2 == 1, (e + 1) // 2, n - e // 2) + k
    place = where(place >= n, place - n, place)
    return where(place == 0, 0, where(place <= n // 2, 2 * place - 1, 2 * (n - place)))


def join(parts):
    top = functools.reduce(jnp.maximum, [p[-1] for p in parts])
    total = sum(p[:-1] * jnp.exp(p[-1] - top)[None] for p in parts)
    return jnp.concatenate([total, top[None]], axis=0)


def dispatch_kernel(chunks, tokens_hbm, params_hbm, w_in_hbm, logits_ref, mine_ref, theirs_ref, w_in_ref,
                    tokens_ref, params_ref, sums_ref, sems):
    core, expert = lax.axis_index("seq") % 2, lax.axis_index("expert")
    groups, tiles, rows, _ = mine_ref.shape
    half = tiles - 2
    slots, width = params_hbm.shape
    copies = [pltpu.make_async_copy(params_hbm, params_ref, sems.at[0])]
    for start, stop in chunks:
        own = pl.ds(start, stop - start)
        copies.append(pltpu.make_async_copy(tokens_hbm.at[own], tokens_ref.at[own], sems.at[len(copies)]))
    copies.append(pltpu.make_async_copy(w_in_hbm, w_in_ref, sems.at[len(copies)]))
    for copy in copies:
        copy.start()
    copies[0].wait()
    params = jnp.concatenate(pieces(params_ref[...], 3), axis=0)
    for copy in copies[1:-1]:
        copy.wait()
    token_high, token_low, rest = pieces(tokens_ref[...], 3)
    nt = ((1,), (1,))
    a = mm(params, token_high, nt)
    b = mm(params[:2 * slots], token_low, nt)
    c = mm(params[:slots], rest, nt)
    small = a[2 * slots:] + b[slots:] + c
    logits = (small + (a[slots:2 * slots] + b[:slots])) + a[:slots]
    logits_ref[...] = logits
    peak = jnp.max(logits, axis=1, keepdims=True)
    weights = jnp.exp(logits - peak)
    mass = jnp.sum(weights, axis=1, keepdims=True)
    weight_high, weight_low = pieces(weights, 2)
    high = mm(jnp.concatenate([weight_high, weight_low], axis=0), token_high)
    low = mm(weight_high, token_low)
    sums_ref[:, :width] = high[:slots] + (high[slots:] + low)
    sums_ref[:, width:width + LANES] = jnp.broadcast_to(mass, (slots, LANES))
    sums_ref[:, width + LANES:] = jnp.broadcast_to(peak, (slots, LANES))
    for k in range(groups):
        target = ring_step(expert, k, groups, jnp.where)
        own = pl.ds(pl.multiple_of(target * rows, rows), rows)
        sides = (core, 1 - core) if k else (1 - core, core)
        for ref, side in zip((mine_ref, theirs_ref), sides):
            for t in range(half):
                place = pl.ds(pl.multiple_of((side * half + t) * LANES, LANES), LANES)
                ref[k, t] = sums_ref[own, place]
            for t in range(2):
                ref[k, half + t] = sums_ref[own, width + t * LANES:width + (t + 1) * LANES]
    copies[-1].wait()


def chip_kernel(mine_ref, theirs_ref, *outs):
    for k, out_ref in enumerate(outs):
        out_ref[...] = join([mine_ref[k], theirs_ref[k]])


def split_out_kernel(_, w_hbm, high_ref, low_ref, flag_ref, w_ref, sems):
    experts, units, _ = w_hbm.shape
    parts = sems.shape[0] // experts
    count = units // parts
    copies = []
    for e in range(experts):
        for i in range(parts):
            own = pl.ds(i * count, count)
            copies.append(pltpu.make_async_copy(w_hbm.at[e, own], w_ref.at[e, own], sems.at[len(copies)]))
            copies[-1].start()
    for e in range(experts):
        for i in range(parts):
            copies[e * parts + i].wait()
            start = e * units + i * count
            own = slice(start, start + count)
            high_ref[own], low_ref[own] = pieces(w_ref[e, i * count:(i + 1) * count], 2)
    flag_ref[...] = jnp.zeros_like(flag_ref)


def split_in_kernel(_, w_ref, high_ref, low_ref, flag_ref):
    experts, units, width = w_ref.shape
    high, low = pieces(w_ref[...].reshape(experts * units, width), 2)
    high_ref[...] = high.T
    low_ref[...] = low.T
    flag_ref[...] = jnp.zeros_like(flag_ref)


def total_kernel(own_ref, *refs):
    *others, _, out_ref = refs
    out_ref[...] = join([own_ref[...]] + [r[...] for r in others])


def plane_kernel(own_ref, *refs):
    *others, _, out_ref = refs
    out_ref[0] = join([r[...] for r in others])
    out_ref[1] = own_ref[...]


def halves_kernel(mine_ref, theirs_ref, keep_ref, send_ref):
    core = lax.axis_index("seq") % 2
    half = keep_ref.shape[0]
    for ref, side in ((send_ref, core), (keep_ref, 1 - core)):
        own = pl.ds(side * half, half)
        ref[...] = mine_ref[own] + theirs_ref[own]


def add_kernel(own_ref, *refs):
    *others, out_ref = refs
    out_ref[...] = own_ref[...] + sum(r[...] for r in others)


def stack_kernel(*refs):
    _, *others, _, out_ref = refs
    for k, r in enumerate(others):
        out_ref[k] = r[...]


def combine_kernel(logits_ref, out_ref):
    logits = logits_ref[...]
    top = jnp.max(logits, axis=0, keepdims=True)
    powers = jnp.exp(logits - top)
    combine = (powers / jnp.sum(powers, axis=0, keepdims=True)).T
    high, low = pieces(combine, 2)
    out_ref[...] = jnp.concatenate([high, low, high], axis=1)


def expert_kernel(sent_ref, got_ref, in_high_ref, in_low_ref, out_high_ref, out_low_ref, out_ref):
    core = lax.axis_index("seq") % 2
    tiles, rows, _ = out_ref.shape
    half = tiles // 2
    experts = rows // SLOTS
    units = in_high_ref.shape[1] // experts
    near = join([sent_ref[0], got_ref[1]])
    far = join([sent_ref[1], got_ref[0]])
    near = [near[t] / near[half] for t in range(half)]
    far = [far[t] / far[half] for t in range(half)]
    first = [pick(core, a, b) for a, b in zip(near, far)]
    second = [pick(core, b, a) for a, b in zip(near, far)]
    inputs = stacked(jnp.concatenate(first + second, axis=1))
    large = mm(inputs, in_high_ref[...])
    small = mm(inputs, in_low_ref[...])
    value = large[:rows] + (large[rows:] + small[:rows])
    value = value * (1.0 + lax.erf(value * (0.5 ** 0.5))) * 0.5
    slot = lax.broadcasted_iota(jnp.int32, value.shape, 0)
    unit = lax.broadcasted_iota(jnp.int32, value.shape, 1)
    keep = None
    for e in range(experts):
        inside = (slot // SLOTS == e) & (unit >= e * units) & (unit < (e + 1) * units)
        keep = inside if keep is None else keep | inside
    hidden = stacked(jnp.where(keep, value, 0.0))
    large = mm(hidden, out_high_ref[...])
    small = mm(hidden, out_low_ref[...])
    out = large[:rows] + (large[rows:] + small[:rows])
    for t in range(tiles):
        out_ref[t] = out[:, t * LANES:(t + 1) * LANES]


def mix_kernel(near, combine_ref, own_ref, others_ref, *refs):
    out_hbm, slots_ref, out_ref, sems = refs[-4:]
    core, expert = lax.axis_index("seq") % 2, lax.axis_index("expert")
    half, rows, _ = own_ref.shape
    groups = others_ref.shape[0] + 1
    for k in range(groups):
        place = pl.ds(pl.multiple_of(lax.rem(expert - k + groups, groups) * rows, rows), rows)
        for t in range(half):
            slots_ref[place, t * LANES:(t + 1) * LANES] = others_ref[k - 1, t] if k else own_ref[t]
    high, low = pieces(slots_ref[...], 2)
    slots = jnp.concatenate([high, high, low], axis=0)
    side = core if near else 1 - core
    columns = pl.ds(pl.multiple_of(side * (half * LANES), LANES), half * LANES)
    count = combine_ref.shape[0]
    step = pl.cdiv(count, 16 * sems.shape[0]) * 16
    copies = []
    for i, start in enumerate(range(0, count, step)):
        size = min(step, count - start)
        out_ref[start:start + size] = mm(combine_ref[start:start + size], slots)
        place = pl.ds(start, size)
        copies.append(pltpu.make_async_copy(out_ref.at[place], out_hbm.at[place, columns], sems.at[i]))
        copies[i].start()
    for copy in copies:
        copy.wait()


def solution(mesh):
    n_expert, n_seq, n_fsdp = (mesh.shape[a] for a in AXES)
    n_x = n_seq // 2

    def permute(value, target):
        pairs = []
        for e in range(n_expert):
            for s in range(n_seq):
                for f in range(n_fsdp):
                    te, tx, tc, tf = target(e, s // 2, s % 2, f)
                    pairs.append(((e * n_seq + s) * n_fsdp + f, (te * n_seq + tx * 2 + tc) * n_fsdp + tf))
        return lax.ppermute(value, AXES, pairs)

    def other_core(value):
        return permute(value, lambda e, x, c, f: (e, x, 1 - c, f))

    def along_ring(value, k):
        return permute(value, lambda e, x, c, f: (ring_step(e, k, n_expert), x, 1 - c, f))

    def around_expert(value, k):
        return permute(value, lambda e, x, c, f: ((e + k) % n_expert, x, 1 - c, f))

    def plane(value):
        return [
            permute(value, lambda e, x, c, f, dx=dx, df=df: (e, (x + dx) % n_x, 1 - c, (f + df) % n_fsdp))
            for dx in range(n_x)[::-1] for df in range(n_fsdp)[::-1] if dx or df
        ]

    def body(tokens, slot_params, w_in, w_out):
        count, width = tokens.shape
        slots = slot_params.shape[1]
        rows = w_in.shape[0] * SLOTS
        half = width // LANES // 2
        f32 = jnp.float32
        params = pltpu.CompilerParams(vmem_limit_bytes=24 * 1024 * 1024)
        core = lax.axis_index("seq") % 2
        step = count // 4 if count % 32 == 0 else count
        chunks = [(i, i + step) for i in range(0, count, step)]
        in_hbm = lambda value: pltpu.with_memory_space_constraint(value, pltpu.HBM)
        shape = pltpu.VMEM((n_expert, half + 2, rows, LANES), f32)
        logits, mine, theirs, w_in = pl.pallas_call(
            functools.partial(dispatch_kernel, chunks),
            out_shape=(pltpu.VMEM((slots, count), f32), shape, shape, pltpu.VMEM(w_in.shape, f32)),
            in_specs=[HBM, HBM, HBM],
            out_specs=(VMEM,) * 4,
            scratch_shapes=[
                pltpu.VMEM((count, width), f32),
                pltpu.VMEM((slots, width), f32),
                pltpu.VMEM((slots, width + 2 * LANES), f32),
                pltpu.SemaphoreType.DMA((len(chunks) + 2,)),
            ],
            compiler_params=params,
        )(in_hbm(tokens), in_hbm(slot_params.T), in_hbm(w_in))
        combine = pl.pallas_call(
            combine_kernel,
            out_shape=jax.ShapeDtypeStruct((count, 3 * slots), jnp.bfloat16),
            in_specs=[VMEM],
            out_specs=VMEM,
            compiler_params=params,
        )(logits)

        chip = pl.pallas_call(
            chip_kernel,
            out_shape=(pltpu.VMEM((half + 2, rows, LANES), f32),) * n_expert,
            in_specs=[VMEM, VMEM],
            out_specs=(VMEM,) * n_expert,
            compiler_params=params,
        )(mine, other_core(theirs))
        flag = pltpu.VMEM((8, LANES), f32)
        experts, units, _ = w_in.shape
        cost = pl.CostEstimate(flops=8 * w_in.size, bytes_accessed=8 * w_in.size, transcendentals=0)

        def local(kernel, out, *args):
            return pl.pallas_call(
                kernel,
                out_shape=out,
                in_specs=[VMEM] * len(args),
                out_specs=jax.tree.map(lambda _: VMEM, out),
                compiler_params=params,
            )(*args)

        part = pltpu.VMEM((experts * units, width), jnp.bfloat16)
        parts = 4 if units % 64 == 0 else 1
        out_high, out_low, ready = pl.pallas_call(
            split_out_kernel,
            out_shape=(part, part, flag),
            in_specs=[VMEM, HBM],
            out_specs=(VMEM,) * 3,
            scratch_shapes=[pltpu.VMEM(w_out.shape, f32), pltpu.SemaphoreType.DMA((experts * parts,))],
            cost_estimate=cost,
            compiler_params=params,
        )(chip[0], in_hbm(w_out))
        shape = pltpu.VMEM((half + 2, rows, LANES), f32)
        total = local(total_kernel, shape, chip[0], *[along_ring(chip[k], k) for k in range(1, n_expert)], ready)
        part = pltpu.VMEM((width, experts * units), jnp.bfloat16)
        in_high, in_low, ready = pl.pallas_call(
            split_in_kernel,
            out_shape=(part, part, flag),
            in_specs=[VMEM, VMEM],
            out_specs=(VMEM,) * 3,
            cost_estimate=cost,
            compiler_params=params,
        )(total, w_in)
        shape = pltpu.VMEM((2, half + 2, rows, LANES), f32)
        sent = local(plane_kernel, shape, total, *plane(total), ready)
        shape = pltpu.VMEM((2 * half, rows, LANES), f32)
        partial = local(expert_kernel, shape, sent, other_core(sent), in_high, in_low, out_high, out_low)
        shape = pltpu.VMEM((half, rows, LANES), f32)
        keep, send = local(halves_kernel, (shape, shape), partial, other_core(partial))
        around = plane(send)
        own = local(add_kernel, shape, keep, *around[-1:], *around[:-1])
        arrived = [around_expert(own, k) for k in range(1, n_expert)]
        own_near = other_core(own)
        shape = pltpu.VMEM((n_expert - 1, half, rows, LANES), f32)
        others = local(stack_kernel, shape, combine, *arrived, own_near)

        def mix(near, own, others, *out):
            return pl.pallas_call(
                functools.partial(mix_kernel, near),
                out_shape=jax.ShapeDtypeStruct((count, width), f32),
                in_specs=[VMEM, VMEM, VMEM] + [HBM] * len(out),
                out_specs=HBM,
                scratch_shapes=[
                    pltpu.VMEM((slots, half * LANES), f32),
                    pltpu.VMEM((count, half * LANES), f32),
                    pltpu.SemaphoreType.DMA((4,)),
                ],
                input_output_aliases={3: 0} if out else {},
                compiler_params=params,
            )(combine, own, others, *out)

        mixed = mix(True, own_near, others)
        return mix(False, own, other_core(others), mixed)

    return jax.shard_map(
        body,
        mesh=mesh,
        in_specs=(P(AXES, None), P(), P("expert", ("seq", "fsdp"), None), P("expert", ("seq", "fsdp"), None)),
        out_specs=P(AXES, None),
        check_vma=False,
    )
```
